512 devices in a mesh: dp: 64 (over x, z_lo, y), mp: 8 (over z_hi, core).
Axes of the slice: x: 4, y: 8, z: 8 (z_hi: 4, z_lo: 2; z = z_hi * 2 + z_lo), core: 2. Of those that a mesh axis runs over, the one named last changes fastest.
Arguments:
- tokens: bfloat16 [81920, 5120], P('dp', 'mp')
- key_weight: bfloat16 [512, 5120], P(None, 'mp'), may hold values from -0.078125 to 0.078125
- key_gain: float32 [512], replicated, may hold values from 0.1 to 1.9
- cotangent: bfloat16 [81920, 512], P('dp', 'mp'), may hold values from -6 to 6
- momentum: bfloat16 [64, 512, 5120], P('dp', None, 'mp')
- band_row: int32 [8, 80], P(None, 'mp'), may hold values from 0 to 3
- band_col: int32 [8, 80], P(None, 'mp'), may hold values from 0 to 3
Outputs:
- update: bfloat16 [512, 5120], P(None, 'mp')
- new_momentum: bfloat16 [64, 512, 5120], P('dp', None, 'mp')
The draws below stay inside these ranges and needn't reach their ends.
Inputs may be any that keep to these rules, and one draw needn't show every extreme that they name: band_row and band_col are the same on every replica; the transform's bands stand at low frequencies.
All inputs are finite; a program needn't handle non-finite values.
Results may differ from the reference program's by a relative error of at most 0.0075.
Values may be sent and summed in bfloat16 or wider, within the bound.
A program may use at most 64 MiB of HBM per device.

```python
import math
import jax
import jax.numpy as jnp
from jax import lax

D = 5120
KV = 512
TOK_DEV = 1280
SPAN = 64
BAND = 8
OFFSETS = 4
BANDS = 8
REPLICAS = 64
TOKENS = 81920
N_DP = 64
N_MP = 8


def draw_tokens(key, part):
    key = jax.random.fold_in(key, 11)
    first_key, second_key = jax.random.split(key, 2)
    values = jax.random.normal(first_key, (TOKENS, D), jnp.float32)
    scales = jnp.exp(jax.random.uniform(second_key, (TOKENS, 1), jnp.float32, jnp.log(0.3), jnp.log(3.0)))
    return (values * scales).astype(jnp.bfloat16)


def draw_momentum(key, part):
    key = jax.random.fold_in(key, 23)
    first_key, second_key = jax.random.split(key, 2)
    shared = jax.random.normal(first_key, (1, KV, D), jnp.float32)
    own_part = jax.random.normal(second_key, (REPLICAS, KV, D), jnp.float32)
    values = 0.7 * shared + 0.7 * own_part
    return values.astype(jnp.bfloat16)


def place_ends(result, rng, smallest, high):
    place = [jax.random.randint(jax.random.fold_in(rng, axis), (), 0, length) for axis, length in enumerate(result.shape)]
    longest = result.shape.index(max(result.shape))
    beside = place[:longest] + [(place[longest] + 1) % result.shape[longest]] + place[longest + 1:]
    return result.at[tuple(place)].set(smallest).at[tuple(beside)].set(high)


def shard_levels(own_key, extent, cuts, least, top_value):
    loudness, own = 1.0, jax.random.fold_in(own_key, 6)
    for dim, blocks in cuts:
        draws = jnp.exp(jax.random.uniform(jax.random.fold_in(own, dim), (blocks,), jnp.float32, least / len(cuts), top_value / len(cuts)))
        loudness = loudness * jnp.repeat(draws, extent[dim] // blocks).reshape([-1 if axis == dim else 1 for axis in range(len(extent))])
    return loudness


def scatter_about(own_key, shape, width, reach, cuts=(), kind=jnp.bfloat16):
    entries = jax.random.normal(own_key, shape, jnp.float32) * width
    if len(cuts) > 0:
        entries = shard_levels(own_key, shape, cuts, -0.22, 0.18) * entries
    return jnp.clip(entries, min=-reach, max=reach).astype(kind)


def setup_inputs(seed: int = 0) -> dict:
    seeds = jax.random.split(jax.random.key(seed), 8)
    tokens = draw_tokens(jax.random.fold_in(seeds[7], 71), 0)
    key_weight = scatter_about(seeds[1], (KV, D), D ** -0.5, 0.078125, ((1, 8),))
    key_gain = jnp.clip(1.0 + 0.18 * jax.random.normal(seeds[2], (KV,), jnp.float32), 0.1, 1.9)
    cotangent = scatter_about(seeds[3], (TOKENS, KV), 1.0, 6.0, ((0, 64), (1, 8)))
    momentum = draw_momentum(jax.random.fold_in(seeds[7], 71), 0)
    band_row = place_ends(jax.random.randint(seeds[5], (KV // SPAN, D // SPAN), 0, OFFSETS), jax.random.fold_in(seeds[5], 1), 0, OFFSETS - 1).astype(jnp.int32)
    band_col = place_ends(jax.random.randint(seeds[6], (KV // SPAN, D // SPAN), 0, OFFSETS), jax.random.fold_in(seeds[6], 1), 0, OFFSETS - 1).astype(jnp.int32)
    return dict(tokens=tokens, key_weight=key_weight, key_gain=key_gain, cotangent=cotangent, momentum=momentum, band_row=band_row, band_col=band_col)


EPS = 1e-06
DECAY = 0.9

def dct_table():
    frequency = jnp.arange(SPAN, dtype=jnp.float32)[:, None]
    position = jnp.arange(SPAN, dtype=jnp.float32)[None, :]
    cosines = jnp.cos(jnp.pi * (2.0 * position + 1.0) * frequency / (2.0 * SPAN))
    row_norms = jnp.where(frequency == 0, jnp.sqrt(1.0 / SPAN), jnp.sqrt(2.0 / SPAN))
    return cosines * row_norms

def band_coeffs(blocks, row_basis, col_basis):
    first_section = jnp.einsum('rckn,rncp->rckp', row_basis, blocks, precision=lax.Precision.HIGHEST)
    return jnp.einsum('rckp,rclp->rckl', first_section, col_basis, precision=lax.Precision.HIGHEST)

def band_rebuild(coeffs, row_basis, col_basis):
    first_section = jnp.einsum('rckl,rclp->rckp', coeffs, col_basis, precision=lax.Precision.HIGHEST)
    return jnp.einsum('rckn,rckp->rncp', row_basis, first_section, precision=lax.Precision.HIGHEST)

def reference(tokens, key_weight, key_gain, cotangent, momentum, band_row, band_col):
    band_basis = dct_table().reshape(BANDS, BAND, SPAN)
    row_basis = band_basis[band_row]
    col_basis = band_basis[band_col]
    rows_blk = KV // SPAN
    cols_blk = D // SPAN
    weight_split = key_weight.astype(jnp.float32).reshape(KV, N_MP, D // N_MP)

    def replica(number):
        offset = number * TOK_DEV
        replica_tokens = lax.dynamic_slice_in_dim(tokens, offset, TOK_DEV, 0)
        cot_rows = lax.dynamic_slice_in_dim(cotangent, offset, TOK_DEV, 0).astype(jnp.float32)
        state_old = lax.dynamic_index_in_dim(momentum, number, 0, keepdims=False).astype(jnp.float32)
        split_tokens = replica_tokens.astype(jnp.float32).reshape(TOK_DEV, N_MP, D // N_MP)
        partial_value = jnp.einsum('tjd,kjd->jtk', split_tokens, weight_split)
        rounded = lax.optimization_barrier(partial_value.astype(jnp.bfloat16)).astype(jnp.float32)
        key_rows = lax.optimization_barrier(jnp.sum(rounded, axis=0))
        inverse = lax.rsqrt(lax.optimization_barrier(jnp.mean(key_rows * key_rows, axis=-1, keepdims=True)) + EPS)
        scaled = key_gain * cot_rows
        inner_sum = lax.optimization_barrier(jnp.sum(scaled * key_rows, axis=-1, keepdims=True))
        dkeys = (inverse * scaled - inverse ** 3 * key_rows * inner_sum / KV).astype(jnp.bfloat16)
        gradient = lax.dot_general(dkeys, replica_tokens, (((0,), (0,)), ((), ())), preferred_element_type=jnp.float32) / math.sqrt(TOK_DEV)
        momentum_new = DECAY * state_old + gradient
        blocks = momentum_new.reshape(rows_blk, SPAN, cols_blk, SPAN)
        coeffs = band_coeffs(blocks, row_basis, col_basis)
        own_part = band_rebuild(coeffs, row_basis, col_basis).reshape(KV, D)
        return ((momentum_new - own_part).astype(jnp.bfloat16), coeffs)
    new_momentum, all_coeffs = lax.map(replica, jnp.arange(N_DP, dtype=jnp.int32))
    averaged = lax.optimization_barrier(jnp.sum(all_coeffs, axis=0)) / N_DP
    update = band_rebuild(averaged, row_basis, col_basis).reshape(KV, D).astype(jnp.bfloat16)
    return (update, new_momentum)
```

```python
import math

import jax
import jax.numpy as jnp
import ml_dtypes
import numpy as np
from jax import lax
from jax.experimental import pallas as pl
from jax.experimental.pallas import tpu as pltpu
from jax.sharding import PartitionSpec as P

MESH = pl.DeviceIdType.MESH
BF = jnp.bfloat16
F32 = jnp.float32

SPAN = 64
BAND = 8
OFFSETS = 4
LOW = BAND * OFFSETS
EPS = 1e-06
DECAY = 0.9

NY = 8
NXZ = 8
NZ = 4
N_DP = NY * NXZ
OWN = 160
KV = 512
WIDTH = 640
ROWS_BLK = KV // SPAN
COLS_BLK = WIDTH // SPAN
LANES = 128
CHUNKS = ((0, 80), (80, 80))


def split_const(table):
    high = table.astype(np.float32).astype(ml_dtypes.bfloat16)
    low = (table - high.astype(np.float64)).astype(np.float32).astype(ml_dtypes.bfloat16)
    return high, low


def tables():
    f = np.arange(SPAN, dtype=np.float64)[:, None]
    n = np.arange(SPAN, dtype=np.float64)[None, :]
    c = np.cos(np.pi * (2.0 * n + 1.0) * f / (2.0 * SPAN))
    c = c * np.where(f == 0, np.sqrt(1.0 / SPAN), np.sqrt(2.0 / SPAN))
    c = c[:LOW]
    left = np.kron(np.eye(4), c)
    right = np.zeros((COLS_BLK, SPAN, OFFSETS, LANES))
    for block in range(COLS_BLK):
        for band in range(OFFSETS):
            right[block, :, band, block * BAND : (block + 1) * BAND] = c[band * BAND : (band + 1) * BAND].T
    right = right.reshape(WIDTH, OFFSETS * LANES)
    lh, ll = split_const(left)
    rh, rl = split_const(right)
    return (
        np.concatenate([lh, ll], axis=0),
        np.stack([np.ascontiguousarray(lh.T), np.ascontiguousarray(ll.T)]),
        np.stack([rh, rl]),
    )


def dot(a, b, dims=((1,), (0,))):
    return lax.dot_general(a, b, (dims, ((), ())), preferred_element_type=F32)


def split(value):
    high = value.astype(BF)
    return high, (value - high.astype(F32)).astype(BF)


def kernel(
    x_hbm, w_hbm, gain_ref, cot_hbm, mom_hbm, row_ref, col_ref, left_hbm, left_t_hbm, right_hbm,
    upd_hbm, new_hbm,
    xv, wv, cotv, momv, leftv, left_tv, rightv,
    cot_sib, cot_mix, cot_all, part_out, part_own, part_in, pair, recv, dk, mom_new,
    row_mask, col_mask, band_y, band_xz, upd_v, new_v,
    load_sem, out_sem, cs_s, cs_r, cz_s, cz_r, ps_s, ps_r, rs_s, rs_r, ag_s, ag_r, fw_s, fw_r,
    y_s, y_r, xz_s, xz_r,
):
    dp = lax.axis_index("dp")
    mp = lax.axis_index("mp")
    zh = mp // 2
    core = mp % 2
    y = dp % NY
    xz = dp // NY
    sib = {"dp": dp, "mp": zh * 2 + (1 - core)}

    def z_peer(step):
        return {"dp": dp, "mp": ((zh + step) % NZ) * 2 + core}

    def y_peer(step):
        return {"dp": xz * NY + (y + step) % NY, "mp": mp}

    def xz_peer(step):
        return {"dp": ((xz + step) % NXZ) * NY + y, "mp": mp}

    barrier = pltpu.get_barrier_semaphore()
    peers = [y_peer(s) for s in (4, 3, 5, 2, 6, 1, 7)] + [xz_peer(s) for s in range(1, NXZ)]
    peers += [z_peer(s) for s in (2, 1, 3)] + [sib]
    for peer in peers:
        pl.semaphore_signal(barrier, inc=1, device_id=peer, device_id_type=MESH)

    loads = [pltpu.make_async_copy(w_hbm, wv, load_sem.at[0])]
    for k, (off, rows) in enumerate(CHUNKS):
        at = (slice(None), slice(None), pl.ds(off, rows))
        loads.append(pltpu.make_async_copy(x_hbm.at[at], xv.at[at], load_sem.at[1 + k]))
    base = 1 + len(CHUNKS)
    more = [(cot_hbm, cotv), (mom_hbm, momv), (left_hbm, leftv), (left_t_hbm, left_tv), (right_hbm, rightv)]
    for k, (src, dst) in enumerate(more):
        loads.append(pltpu.make_async_copy(src, dst, load_sem.at[base + k]))
    for load in loads:
        load.start()

    def remote(src, dst, send, recv_, peer):
        return pltpu.make_async_remote_copy(
            src_ref=src, dst_ref=dst, send_sem=send, recv_sem=recv_, device_id=peer, device_id_type=MESH
        )

    sent = []

    def start(copy):
        copy.start()
        sent.append(copy)

    loads[0].wait()
    for k, (off, rows) in enumerate(CHUNKS):
        loads[1 + k].wait()
        at = pl.ds(off, rows)
        for side, place in ((1 - core, part_out), (core, part_own)):
            x_rows = xv[:, side, at, :].reshape(NZ * rows, WIDTH)
            part = dot(x_rows, wv[...], ((1,), (1,)))
            place[:, at, :] = part.astype(BF).reshape(NZ, rows, KV)

    loads[base].wait()
    pl.semaphore_wait(barrier, len(peers))

    cot_swap = remote(cotv.at[:, 1 - core], cot_sib, cs_s, cs_r, sib)
    start(cot_swap)
    part_swaps = []
    for k, (off, rows) in enumerate(CHUNKS):
        at = (slice(None), pl.ds(off, rows))
        part_swaps.append(remote(part_out.at[at], part_in.at[at], ps_s.at[k], ps_r.at[k], sib))
        start(part_swaps[-1])

    cot_swap.wait_recv()
    feature = lax.broadcasted_iota(jnp.int32, (SPAN, LANES), 0)
    lane = lax.broadcasted_iota(jnp.int32, (SPAN, LANES), 1)
    put_own = (lane == feature + core * SPAN).astype(BF)
    put_sib = (lane == feature + (1 - core) * SPAN).astype(BF)
    mixed = dot(cotv[:, core].reshape(NZ * OWN, SPAN), put_own) + dot(cot_sib[...].reshape(NZ * OWN, SPAN), put_sib)
    cot_mix[...] = mixed.astype(BF).reshape(NZ, OWN, LANES)
    cot_all[zh] = cot_mix[zh]
    for step in (2, 1, 3):
        start(remote(
            cot_mix.at[(zh + step) % NZ], cot_all.at[zh], cz_s.at[step - 1], cz_r.at[step - 1], z_peer(step)
        ))

    for k, (off, rows) in enumerate(CHUNKS):
        at = pl.ds(off, rows)
        part_swaps[k].wait_recv()
        pair[:, at, :] = (part_own[:, at, :].astype(F32) + part_in[:, at, :].astype(F32)).astype(BF)
        for step in (2, 1, 3):
            start(remote(
                pair.at[(zh + step) % NZ, at], recv.at[step - 1, at],
                rs_s.at[k, step - 1], rs_r.at[k, step - 1], z_peer(step),
            ))

    block_r = lax.broadcasted_iota(jnp.int32, (BAND, WIDTH), 1) // SPAN
    block_c = lax.broadcasted_iota(jnp.int32, (BAND, LANES), 1) // BAND

    def spread(r, carry):
        of_row = jnp.zeros((BAND, WIDTH), jnp.int32)
        of_col = jnp.zeros((BAND, LANES), jnp.int32)
        for c in range(COLS_BLK):
            of_row = jnp.where(block_r == c, row_ref[r, c], of_row)
            of_col = jnp.where(block_c == c, col_ref[r, c], of_col)
        row_mask[r] = of_row
        col_mask[r] = of_col
        return carry

    lax.fori_loop(0, ROWS_BLK, spread, 0)
    for load in loads[base + 1 :]:
        load.wait()
    mom_new[...] = DECAY * momv[0].astype(F32)

    for step in (2, 1, 3):
        src = (zh + NZ - step) % NZ
        remote(cot_mix.at[0], cot_all.at[src], cz_s.at[step - 1], cz_r.at[step - 1], sib).wait_recv()
    gain = gain_ref[...]
    for k, (off, rows) in enumerate(CHUNKS):
        at = pl.ds(off, rows)
        keys = pair[zh, at, :].astype(F32)
        for step in (1, 3, 2):
            remote(pair.at[0, at], recv.at[step - 1, at], rs_s.at[k, step - 1], rs_r.at[k, step - 1], sib).wait_recv()
            keys = keys + recv[step - 1, at, :].astype(F32)
        scaled = gain * jnp.concatenate([cot_all[j, at, :].astype(F32) for j in range(NZ)], axis=-1)
        inverse = lax.rsqrt(jnp.mean(keys * keys, axis=-1, keepdims=True) + EPS)
        inner = jnp.sum(scaled * keys, axis=-1, keepdims=True)
        dk[mp, at, :] = (inverse * scaled - (inverse * inverse * inverse * inner / KV) * keys).astype(BF)
        for step in (2, 1, 3):
            start(remote(dk.at[mp, at], dk.at[mp, at], ag_s.at[k, step - 1], ag_r.at[k, step - 1], z_peer(step)))
        start(remote(dk.at[mp, at], dk.at[mp, at], fw_s.at[k, 0], fw_r.at[k, 0], sib))

    for k, (off, rows) in enumerate(CHUNKS):
        at = pl.ds(off, rows)
        for step in (1, 3, 2):
            src = ((zh + NZ - step) % NZ) * 2 + core
            got = dk.at[src, at]
            remote(got, got, ag_s.at[k, step - 1], ag_r.at[k, step - 1], sib).wait_recv()
            start(remote(got, got, fw_s.at[k, step], fw_r.at[k, step], sib))
        for step in (0, 1, 3, 2):
            got = dk.at[((zh + NZ - step) % NZ) * 2 + 1 - core, at]
            remote(got, got, fw_s.at[k, step], fw_r.at[k, step], sib).wait_recv()
        all_dk = dk[:, at, :].reshape(2 * NZ * rows, KV)
        all_x = xv[:, :, at, :].reshape(2 * NZ * rows, WIDTH)
        mom_new[...] += dot(all_dk, all_x, ((0,), (0,))) * (1.0 / math.sqrt(2 * NZ * OWN))

    picked = []
    for g in range(2):
        high, low = split(mom_new[g * 256 : (g + 1) * 256, :])
        both = dot(leftv[...], high)
        sect = both[:128] + both[128:] + dot(leftv[:128], low)
        sect = sect.reshape(4, OFFSETS, BAND, WIDTH)
        chosen = row_mask[g * 4 : (g + 1) * 4]
        total = jnp.zeros((4, BAND, WIDTH), F32)
        for band in range(OFFSETS):
            total = total + jnp.where(chosen == band, sect[:, band], 0.0)
        picked.append(total.reshape(32, WIDTH))
    sect = jnp.concatenate(picked, axis=0)
    high, low = split(sect)
    both = dot(jnp.concatenate([high, low], axis=0), rightv[0])
    full = both[:64] + both[64:] + dot(high, rightv[1])
    chosen = col_mask[...].reshape(64, LANES)
    coeffs = jnp.zeros((64, LANES), F32)
    for band in range(OFFSETS):
        coeffs = coeffs + jnp.where(chosen == band, full[:, band * LANES : (band + 1) * LANES], 0.0)

    band_y[y] = coeffs.astype(BF)
    for step in (4, 3, 5, 2, 6, 1, 7):
        start(remote(band_y.at[y], band_y.at[y], y_s.at[step - 1], y_r.at[step - 1], y_peer(step)))

    def rebuild(values, put):
        parts = [jnp.where(chosen == band, values, 0.0) for band in range(OFFSETS)]
        high, low = split(jnp.concatenate(parts, axis=1))
        both = dot(jnp.concatenate([high, low], axis=0), rightv[0], ((1,), (1,)))
        first = both[:64] + both[64:] + dot(high, rightv[1], ((1,), (1,)))
        for g in range(2):
            rows = first[g * 32 : (g + 1) * 32].reshape(4, 1, BAND, WIDTH)
            bands = lax.broadcasted_iota(jnp.int32, (4, OFFSETS, BAND, WIDTH), 1)
            mask = row_mask[g * 4 : (g + 1) * 4].reshape(4, 1, BAND, WIDTH)
            spread_rows = jnp.where(mask == bands, rows, 0.0).reshape(128, WIDTH)
            high, low = split(spread_rows)
            out = dot(left_tv[0], high) + dot(left_tv[1], high) + dot(left_tv[0], low)
            put(g, out)

    def put_new(g, own):
        at = slice(g * 256, (g + 1) * 256)
        new_v[0, at, :] = (mom_new[at, :] - own).astype(BF)

    rebuild(coeffs, put_new)
    store_new = pltpu.make_async_copy(new_v, new_hbm, out_sem.at[0])
    store_new.start()

    for step in (1, 7, 2, 6, 3, 5, 4):
        got = band_y.at[(y + NY - step) % NY]
        remote(got, got, y_s.at[step - 1], y_r.at[step - 1], sib).wait_recv()
    total = band_y[0].astype(F32)
    for j in range(1, NY):
        total = total + band_y[j].astype(F32)
    band_xz[xz] = total.astype(BF)
    for step in range(1, NXZ):
        start(remote(band_xz.at[xz], band_xz.at[xz], xz_s.at[step - 1], xz_r.at[step - 1], xz_peer(step)))
    for step in range(1, NXZ):
        got = band_xz.at[(xz + NXZ - step) % NXZ]
        remote(got, got, xz_s.at[step - 1], xz_r.at[step - 1], sib).wait_recv()
    total = band_xz[0].astype(F32)
    for j in range(1, NXZ):
        total = total + band_xz[j].astype(F32)

    def put_update(g, value):
        upd_v[g * 256 : (g + 1) * 256, :] = value.astype(BF)

    rebuild(total * (1.0 / N_DP), put_update)
    store_upd = pltpu.make_async_copy(upd_v, upd_hbm, out_sem.at[1])
    store_upd.start()
    for copy in sent:
        copy.wait_send()
    store_new.wait()
    store_upd.wait()


def on_device(tokens, key_weight, key_gain, cotangent, momentum, band_row, band_col):
    left, left_t, right = tables()
    n = len(CHUNKS)
    any_spec = pl.BlockSpec(memory_space=pl.ANY)
    smem = pl.BlockSpec(memory_space=pltpu.SMEM)
    vmem = pl.BlockSpec(memory_space=pltpu.VMEM)
    dma = pltpu.SemaphoreType.DMA
    return pl.pallas_call(
        kernel,
        out_shape=(
            jax.ShapeDtypeStruct((KV, WIDTH), BF),
            jax.ShapeDtypeStruct((1, KV, WIDTH), BF),
        ),
        in_specs=[any_spec, any_spec, vmem, any_spec, any_spec, smem, smem, any_spec, any_spec, any_spec],
        out_specs=(any_spec, any_spec),
        scratch_shapes=[
            pltpu.VMEM((NZ, 2, OWN, WIDTH), BF),
            pltpu.VMEM((KV, WIDTH), BF),
            pltpu.VMEM((NZ, 2, OWN, SPAN), BF),
            pltpu.VMEM((1, KV, WIDTH), BF),
            pltpu.VMEM(left.shape, BF),
            pltpu.VMEM(left_t.shape, BF),
            pltpu.VMEM(right.shape, BF),
            pltpu.VMEM((NZ, OWN, SPAN), BF),
            pltpu.VMEM((NZ, OWN, LANES), BF),
            pltpu.VMEM((NZ, OWN, LANES), BF),
            pltpu.VMEM((NZ, OWN, KV), BF),
            pltpu.VMEM((NZ, OWN, KV), BF),
            pltpu.VMEM((NZ, OWN, KV), BF),
            pltpu.VMEM((NZ, OWN, KV), BF),
            pltpu.VMEM((NZ - 1, OWN, KV), BF),
            pltpu.VMEM((2 * NZ, OWN, KV), BF),
            pltpu.VMEM((KV, WIDTH), F32),
            pltpu.VMEM((ROWS_BLK, BAND, WIDTH), jnp.int32),
            pltpu.VMEM((ROWS_BLK, BAND, LANES), jnp.int32),
            pltpu.VMEM((NY, 64, LANES), BF),
            pltpu.VMEM((NXZ, 64, LANES), BF),
            pltpu.VMEM((KV, WIDTH), BF),
            pltpu.VMEM((1, KV, WIDTH), BF),
            dma((6 + n,)),
            dma((2,)),
            dma(()),
            dma(()),
            dma((3,)),
            dma((3,)),
            dma((n,)),
            dma((n,)),
            dma((n, 3)),
            dma((n, 3)),
            dma((n, 3)),
            dma((n, 3)),
            dma((n, 4)),
            dma((n, 4)),
            dma((7,)),
            dma((7,)),
            dma((7,)),
            dma((7,)),
        ],
        compiler_params=pltpu.CompilerParams(
            collective_id=0, has_side_effects=True, vmem_limit_bytes=48 * 1024 * 1024
        ),
        cost_estimate=pl.CostEstimate(flops=2_500_000_000, bytes_accessed=6_000_000, transcendentals=1280),
    )(
        tokens.reshape(NZ, 2, OWN, WIDTH),
        key_weight,
        key_gain.reshape(1, KV),
        cotangent.reshape(NZ, 2, OWN, SPAN),
        momentum,
        band_row,
        band_col,
        left,
        left_t,
        right,
    )


def solution(mesh):
    return jax.shard_map(
        on_device,
        mesh=mesh,
        in_specs=(
            P("dp", "mp"),
            P(None, "mp"),
            P(),
            P("dp", "mp"),
            P("dp", None, "mp"),
            P(None, "mp"),
            P(None, "mp"),
        ),
        out_specs=(P(None, "mp"), P("dp", None, "mp")),
        check_vma=False,
    )
```

```python
import math

import jax
import jax.numpy as jnp
import ml_dtypes
import numpy as np
from jax import lax
from jax.experimental import pallas as pl
from jax.experimental.pallas import tpu as pltpu
from jax.sharding import PartitionSpec as P

MESH = pl.DeviceIdType.MESH
BF = jnp.bfloat16
F32 = jnp.float32

SPAN = 64
BAND = 8
OFFSETS = 4
LOW = BAND * OFFSETS
EPS = 1e-06
DECAY = 0.9

NY = 8
NXZ = 8
NZ = 4
N_DP = NY * NXZ
OWN = 160
KV = 512
WIDTH = 640
ROWS_BLK = KV // SPAN
COLS_BLK = WIDTH // SPAN
LANES = 128
CHUNKS = ((0, 80), (80, 80))
WAYS = ((1, slice(0, 256)), (3, slice(256, 512)))


def split_const(table):
    high = table.astype(np.float32).astype(ml_dtypes.bfloat16)
    low = (table - high.astype(np.float64)).astype(np.float32).astype(ml_dtypes.bfloat16)
    return high.astype(np.float32), low.astype(np.float32)


def tables():
    f = np.arange(SPAN, dtype=np.float64)[:, None]
    n = np.arange(SPAN, dtype=np.float64)[None, :]
    c = np.cos(np.pi * (2.0 * n + 1.0) * f / (2.0 * SPAN))
    c = c * np.where(f == 0, np.sqrt(1.0 / SPAN), np.sqrt(2.0 / SPAN))
    c = c[:LOW]
    high, low = split_const(np.kron(np.eye(4), c))
    right = np.zeros((SPAN, OFFSETS, LANES // BAND, BAND))
    right[:] = c.T.reshape(SPAN, OFFSETS, 1, BAND)
    return (
        np.concatenate([high, low], axis=0),
        np.stack([np.ascontiguousarray(high.T), np.ascontiguousarray(low.T)]),
        np.stack(split_const(right.reshape(SPAN, OFFSETS * LANES))),
    )


def dot(a, b, dims=((1,), (0,))):
    return lax.dot_general(a, b, (dims, ((), ())), preferred_element_type=F32)


def split(value):
    high = value.astype(BF)
    return high, (value - high.astype(F32)).astype(BF)


def kernel(
    x_hbm, w_hbm, gain_ref, cot_hbm, mom_hbm, row_ref, col_ref, left_hbm, left_t_hbm, right_hbm,
    upd_hbm, new_hbm,
    xv, wv, momv, left_f, left_t_f, right_f, leftv, left_tv, rightv,
    cot_pair, cot_mix, cot_all, part_out, part_own, part_in, pair, relay, relay_sum, recv, dk, mom_new,
    row_mask, col_mask, band_y, band_xz, upd_v, new_v,
    load_sem, out_sem, cs_s, cs_r, cz_s, cz_r, ps_s, ps_r, r1_s, r1_r, rd_s, rd_r, r2_s, r2_r, ag_s, ag_r, a2_s, a2_r, fw_s, fw_r,
    y_s, y_r, xz_s, xz_r,
):
    dp = lax.axis_index("dp")
    mp = lax.axis_index("mp")
    zh = mp // 2
    core = mp % 2
    y = dp % NY
    xz = dp // NY
    sib = {"dp": dp, "mp": zh * 2 + (1 - core)}

    def z_peer(step):
        return {"dp": dp, "mp": ((zh + step) % NZ) * 2 + core}

    def y_peer(step):
        return {"dp": xz * NY + (y + step) % NY, "mp": mp}

    def xz_peer(step):
        return {"dp": ((xz + step) % NXZ) * NY + y, "mp": mp}

    barrier = pltpu.get_barrier_semaphore()
    peers = [y_peer(s) for s in (4, 3, 5, 2, 6, 1, 7)] + [xz_peer(s) for s in range(1, NXZ)]
    peers += [z_peer(s) for s in (2, 1, 3)] + [sib]
    for peer in peers:
        pl.semaphore_signal(barrier, inc=1, device_id=peer, device_id_type=MESH)

    loads = [pltpu.make_async_copy(w_hbm, wv, load_sem.at[0])]
    for k, (off, rows) in enumerate(CHUNKS):
        at = (slice(None), slice(None), pl.ds(off, rows))
        loads.append(pltpu.make_async_copy(x_hbm.at[at], xv.at[at], load_sem.at[1 + k]))
    base = 1 + len(CHUNKS)
    more = [(cot_hbm, cot_pair.at[core]), (mom_hbm, momv)]
    more += [(left_hbm, left_f), (left_t_hbm, left_t_f), (right_hbm, right_f)]
    for k, (src, dst) in enumerate(more):
        loads.append(pltpu.make_async_copy(src, dst, load_sem.at[base + k]))
    for load in loads:
        load.start()

    def remote(src, dst, send, recv_, peer):
        return pltpu.make_async_remote_copy(
            src_ref=src, dst_ref=dst, send_sem=send, recv_sem=recv_, device_id=peer, device_id_type=MESH
        )

    sent = []
    flying = {}

    def start(key, copy):
        copy.start()
        sent.append(copy)
        flying[key] = copy

    def landed(key, copy):
        copy.wait_recv()
        del flying[key]

    part_swaps = []

    def partial_keys(k):
        off, rows = CHUNKS[k]
        loads[1 + k].wait()
        at = pl.ds(off, rows)
        for side, place in ((1 - core, part_out), (core, part_own)):
            x_rows = xv[:, side, at, :].reshape(NZ * rows, WIDTH)
            part = dot(x_rows, wv[...], ((1,), (1,)))
            place[:, at, :] = part.astype(BF).reshape(NZ, rows, KV)

    def swap_parts(k):
        at = (slice(None), pl.ds(*CHUNKS[k]))
        part_swaps.append(remote(part_out.at[at], part_in.at[at], ps_s.at[k], ps_r.at[k], sib))
        start(("ps", k), part_swaps[k])

    loads[0].wait()
    partial_keys(0)
    pl.semaphore_wait(barrier, len(peers))
    swap_parts(0)
    cot_swap = remote(cot_hbm, cot_pair.at[core], cs_s, cs_r, sib)
    start(("cs",), cot_swap)
    for k in range(1, len(CHUNKS)):
        partial_keys(k)
        swap_parts(k)

    for k, (off, rows) in enumerate(CHUNKS):
        at = pl.ds(off, rows)
        landed(("ps", k), part_swaps[k])
        pair[:, at, :] = (part_own[:, at, :].astype(F32) + part_in[:, at, :].astype(F32)).astype(BF)
        for way, (step, half) in enumerate(WAYS):
            start(("r1", k, way), remote(
                pair.at[(zh + 2) % NZ, at, half], relay.at[way, at], r1_s.at[k, way], r1_r.at[k, way], z_peer(step)
            ))

    loads[base].wait()
    landed(("cs",), cot_swap)
    cot_mix[...] = cot_pair[...].reshape(LANES, 2 * NZ * OWN).T.reshape(NZ, 2, OWN, LANES)
    cot_all[zh] = cot_mix[zh, core]
    for step in (2, 1, 3):
        start(("cz", step), remote(
            cot_mix.at[(zh + step) % NZ, core], cot_all.at[zh], cz_s.at[step - 1], cz_r.at[step - 1], z_peer(step)
        ))
    for k, (off, rows) in enumerate(CHUNKS):
        at = pl.ds(off, rows)
        for way, (step, half) in enumerate(WAYS):
            other = WAYS[1 - way][1]
            start(("rd", k, way), remote(
                pair.at[(zh + step) % NZ, at, other], recv.at[way, at, other],
                rd_s.at[k, way], rd_r.at[k, way], z_peer(step),
            ))
    for k, (off, rows) in enumerate(CHUNKS):
        at = pl.ds(off, rows)
        for way, (step, half) in enumerate(WAYS):
            landed(("r1", k, way), remote(
                pair.at[0, at, half], relay.at[way, at], r1_s.at[k, way], r1_r.at[k, way], sib
            ))
            both = pair[(zh + step) % NZ, at, half].astype(F32) + relay[way, at, :].astype(F32)
            relay_sum[way, at, :] = both.astype(BF)
            start(("r2", k, way), remote(
                relay_sum.at[way, at], recv.at[way, at, half], r2_s.at[k, way], r2_r.at[k, way], z_peer(step)
            ))

    block_r = lax.broadcasted_iota(jnp.int32, (BAND, WIDTH), 1) // SPAN
    block_c = lax.broadcasted_iota(jnp.int32, (BAND, LANES), 1) // BAND

    def spread(r, carry):
        of_row = jnp.zeros((BAND, WIDTH), jnp.int32)
        of_col = jnp.zeros((BAND, LANES), jnp.int32)
        for c in range(COLS_BLK):
            of_row = jnp.where(block_r == c, row_ref[r, c], of_row)
            of_col = jnp.where(block_c == c, col_ref[r, c], of_col)
        row_mask[r] = of_row
        col_mask[r] = of_col
        return carry

    lax.fori_loop(0, ROWS_BLK, spread, 0)
    for load in loads[base + 1 :]:
        load.wait()
    mom_new[...] = DECAY * momv[0].astype(F32)
    leftv[...] = left_f[...].astype(BF)
    left_tv[...] = left_t_f[...].astype(BF)
    lane_block = (lax.broadcasted_iota(jnp.int32, (SPAN, OFFSETS * LANES), 1) % LANES) // BAND
    for c in range(COLS_BLK):
        for part in range(2):
            rightv[part, c * SPAN : (c + 1) * SPAN] = jnp.where(lane_block == c, right_f[part], 0.0).astype(BF)

    for step in (2, 1, 3):
        src = (zh + NZ - step) % NZ
        landed(("cz", step), remote(cot_mix.at[0, 0], cot_all.at[src], cz_s.at[step - 1], cz_r.at[step - 1], sib))
    gain = gain_ref[...]
    for k, (off, rows) in enumerate(CHUNKS):
        at = pl.ds(off, rows)
        for way, (step, half) in enumerate(WAYS):
            other = WAYS[1 - way][1]
            landed(("rd", k, way), remote(
                pair.at[0, at, other], recv.at[way, at, other], rd_s.at[k, way], rd_r.at[k, way], sib
            ))
        for way, (step, half) in enumerate(WAYS):
            landed(("r2", k, way), remote(
                relay_sum.at[way, at], recv.at[way, at, half], r2_s.at[k, way], r2_r.at[k, way], sib
            ))
        keys = pair[zh, at, :].astype(F32) + recv[0, at, :].astype(F32) + recv[1, at, :].astype(F32)
        scaled = gain * jnp.concatenate([cot_all[j, at, :].astype(F32) for j in range(NZ)], axis=-1)
        inverse = lax.rsqrt(jnp.mean(keys * keys, axis=-1, keepdims=True) + EPS)
        inner = jnp.sum(scaled * keys, axis=-1, keepdims=True)
        dk[mp, at, :] = (inverse * scaled - (inverse * inverse * inverse * inner / KV) * keys).astype(BF)
        mine = dk.at[mp, at]
        for way, (step, half) in enumerate(WAYS):
            start(("ag", k, way), remote(mine, mine, ag_s.at[k, way], ag_r.at[k, way], z_peer(step)))
        start(("fw", k, 0), remote(mine, mine, fw_s.at[k, 0], fw_r.at[k, 0], sib))

    def owner(step, side):
        return ((zh + NZ - step) % NZ) * 2 + side

    for k, (off, rows) in enumerate(CHUNKS):
        at = pl.ds(off, rows)
        for way, (step, half) in enumerate(WAYS):
            got = dk.at[owner(step, core), at]
            landed(("ag", k, way), remote(got, got, ag_s.at[k, way], ag_r.at[k, way], sib))
            part = dk.at[owner(step, core), at, half]
            start(("a2", k, way), remote(part, part, a2_s.at[k, way], a2_r.at[k, way], z_peer(step)))
            start(("fw", k, step), remote(got, got, fw_s.at[k, step], fw_r.at[k, step], sib))
    for k, (off, rows) in enumerate(CHUNKS):
        at = pl.ds(off, rows)
        for way, (step, half) in enumerate(WAYS):
            part = dk.at[owner(2, core), at, half]
            landed(("a2", k, way), remote(part, part, a2_s.at[k, way], a2_r.at[k, way], sib))
        got = dk.at[owner(2, core), at]
        start(("fw", k, 2), remote(got, got, fw_s.at[k, 2], fw_r.at[k, 2], sib))
        for step in (0, 1, 3, 2):
            got = dk.at[owner(step, 1 - core), at]
            landed(("fw", k, step), remote(got, got, fw_s.at[k, step], fw_r.at[k, step], sib))
        all_dk = dk[:, at, :].reshape(2 * NZ * rows, KV)
        all_x = xv[:, :, at, :].reshape(2 * NZ * rows, WIDTH)
        mom_new[...] += dot(all_dk, all_x, ((0,), (0,))) * (1.0 / math.sqrt(2 * NZ * OWN))

    picked = []
    for g in range(2):
        high, low = split(mom_new[g * 256 : (g + 1) * 256, :])
        both = dot(leftv[...], high)
        sect = both[:128] + both[128:] + dot(leftv[:128], low)
        sect = sect.reshape(4, OFFSETS, BAND, WIDTH)
        chosen = row_mask[g * 4 : (g + 1) * 4]
        total = jnp.zeros((4, BAND, WIDTH), F32)
        for band in range(OFFSETS):
            total = total + jnp.where(chosen == band, sect[:, band], 0.0)
        picked.append(total.reshape(32, WIDTH))
    sect = jnp.concatenate(picked, axis=0)
    high, low = split(sect)
    both = dot(jnp.concatenate([high, low], axis=0), rightv[0])
    full = both[:64] + both[64:] + dot(high, rightv[1])
    chosen = col_mask[...].reshape(64, LANES)
    coeffs = jnp.zeros((64, LANES), F32)
    for band in range(OFFSETS):
        coeffs = coeffs + jnp.where(chosen == band, full[:, band * LANES : (band + 1) * LANES], 0.0)

    band_y[y] = coeffs.astype(BF)
    for step in (4, 3, 5, 2, 6, 1, 7):
        start(("y", step), remote(band_y.at[y], band_y.at[y], y_s.at[step - 1], y_r.at[step - 1], y_peer(step)))

    def rebuild(values, put):
        parts = [jnp.where(chosen == band, values, 0.0) for band in range(OFFSETS)]
        high, low = split(jnp.concatenate(parts, axis=1))
        both = dot(jnp.concatenate([high, low], axis=0), rightv[0], ((1,), (1,)))
        first = both[:64] + both[64:] + dot(high, rightv[1], ((1,), (1,)))
        for g in range(2):
            rows = first[g * 32 : (g + 1) * 32].reshape(4, 1, BAND, WIDTH)
            bands = lax.broadcasted_iota(jnp.int32, (4, OFFSETS, BAND, WIDTH), 1)
            mask = row_mask[g * 4 : (g + 1) * 4].reshape(4, 1, BAND, WIDTH)
            spread_rows = jnp.where(mask == bands, rows, 0.0).reshape(128, WIDTH)
            high, low = split(spread_rows)
            out = dot(left_tv[0], high) + dot(left_tv[1], high) + dot(left_tv[0], low)
            put(g, out)

    def put_new(g, own):
        at = slice(g * 256, (g + 1) * 256)
        new_v[0, at, :] = (mom_new[at, :] - own).astype(BF)

    rebuild(coeffs, put_new)
    store_new = pltpu.make_async_copy(new_v, new_hbm, out_sem.at[0])
    store_new.start()

    for step in (1, 7, 2, 6, 3, 5, 4):
        got = band_y.at[(y + NY - step) % NY]
        landed(("y", step), remote(got, got, y_s.at[step - 1], y_r.at[step - 1], sib))
    total = band_y[0].astype(F32)
    for j in range(1, NY):
        total = total + band_y[j].astype(F32)
    band_xz[xz] = total.astype(BF)
    for step in range(1, NXZ):
        start(("xz", step), remote(band_xz.at[xz], band_xz.at[xz], xz_s.at[step - 1], xz_r.at[step - 1], xz_peer(step)))
    for step in range(1, NXZ):
        got = band_xz.at[(xz + NXZ - step) % NXZ]
        landed(("xz", step), remote(got, got, xz_s.at[step - 1], xz_r.at[step - 1], sib))
    total = band_xz[0].astype(F32)
    for j in range(1, NXZ):
        total = total + band_xz[j].astype(F32)

    def put_update(g, value):
        upd_v[g * 256 : (g + 1) * 256, :] = value.astype(BF)

    rebuild(total * (1.0 / N_DP), put_update)
    store_upd = pltpu.make_async_copy(upd_v, upd_hbm, out_sem.at[1])
    store_upd.start()
    for copy in sent:
        copy.wait_send()
    store_new.wait()
    store_upd.wait()


def on_device(tokens, key_weight, key_gain, cotangent, momentum, band_row, band_col):
    left, left_t, right = tables()
    n = len(CHUNKS)
    any_spec = pl.BlockSpec(memory_space=pltpu.HBM)
    smem = pl.BlockSpec(memory_space=pltpu.SMEM)
    vmem = pl.BlockSpec(memory_space=pltpu.VMEM)
    dma = pltpu.SemaphoreType.DMA
    return pl.pallas_call(
        kernel,
        out_shape=(
            jax.ShapeDtypeStruct((KV, WIDTH), BF),
            jax.ShapeDtypeStruct((1, KV, WIDTH), BF),
        ),
        in_specs=[any_spec, any_spec, vmem, any_spec, any_spec, smem, smem, any_spec, any_spec, any_spec],
        out_specs=(any_spec, any_spec),
        scratch_shapes=[
            pltpu.VMEM((NZ, 2, OWN, WIDTH), BF),
            pltpu.VMEM((KV, WIDTH), BF),
            pltpu.VMEM((1, KV, WIDTH), BF),
            pltpu.VMEM(left.shape, F32),
            pltpu.VMEM(left_t.shape, F32),
            pltpu.VMEM(right.shape, F32),
            pltpu.VMEM(left.shape, BF),
            pltpu.VMEM(left_t.shape, BF),
            pltpu.VMEM((2, WIDTH, OFFSETS * LANES), BF),
            pltpu.VMEM((2, SPAN, 2 * NZ * OWN), BF),
            pltpu.VMEM((NZ, 2, OWN, LANES), BF),
            pltpu.VMEM((NZ, OWN, LANES), BF),
            pltpu.VMEM((NZ, OWN, KV), BF),
            pltpu.VMEM((NZ, OWN, KV), BF),
            pltpu.VMEM((NZ, OWN, KV), BF),
            pltpu.VMEM((NZ, OWN, KV), BF),
            pltpu.VMEM((2, OWN, KV // 2), BF),
            pltpu.VMEM((2, OWN, KV // 2), BF),
            pltpu.VMEM((2, OWN, KV), BF),
            pltpu.VMEM((2 * NZ, OWN, KV), BF),
            pltpu.VMEM((KV, WIDTH), F32),
            pltpu.VMEM((ROWS_BLK, BAND, WIDTH), jnp.int32),
            pltpu.VMEM((ROWS_BLK, BAND, LANES), jnp.int32),
            pltpu.VMEM((NY, 64, LANES), BF),
            pltpu.VMEM((NXZ, 64, LANES), BF),
            pltpu.VMEM((KV, WIDTH), BF),
            pltpu.VMEM((1, KV, WIDTH), BF),
            dma((6 + n,)),
            dma((2,)),
            dma(()),
            dma(()),
            dma((3,)),
            dma((3,)),
            dma((n,)),
            dma((n,)),
            dma((n, 2)),
            dma((n, 2)),
            dma((n, 2)),
            dma((n, 2)),
            dma((n, 2)),
            dma((n, 2)),
            dma((n, 2)),
            dma((n, 2)),
            dma((n, 2)),
            dma((n, 2)),
            dma((n, 4)),
            dma((n, 4)),
            dma((7,)),
            dma((7,)),
            dma((7,)),
            dma((7,)),
        ],
        compiler_params=pltpu.CompilerParams(
            collective_id=0, has_side_effects=True, vmem_limit_bytes=64 * 1024 * 1024
        ),
        cost_estimate=pl.CostEstimate(flops=2_500_000_000, bytes_accessed=6_000_000, transcendentals=1280),
    )(
        tokens.reshape(NZ, 2, OWN, WIDTH),
        key_weight,
        key_gain.reshape(1, KV),
        cotangent.T,
        momentum,
        band_row,
        band_col,
        left,
        left_t,
        right,
    )


def solution(mesh):
    return jax.shard_map(
        on_device,
        mesh=mesh,
        in_specs=(
            P("dp", "mp"),
            P(None, "mp"),
            P(),
            P("dp", "mp"),
            P("dp", None, "mp"),
            P(None, "mp"),
            P(None, "mp"),
        ),
        out_specs=(P(None, "mp"), P("dp", None, "mp")),
        check_vma=False,
    )
```

```python
import math

import jax
import jax.numpy as jnp
import ml_dtypes
import numpy as np
from jax import lax
from jax.experimental import pallas as pl
from jax.experimental.pallas import tpu as pltpu
from jax.sharding import PartitionSpec as P

MESH = pl.DeviceIdType.MESH
BF = jnp.bfloat16
F32 = jnp.float32

SPAN = 64
BAND = 8
OFFSETS = 4
LOW = BAND * OFFSETS
EPS = 1e-06
DECAY = 0.9

NY = 8
NXZ = 8
NZ = 4
N_DP = NY * NXZ
OWN = 160
KV = 512
WIDTH = 640
ROWS_BLK = KV // SPAN
COLS_BLK = WIDTH // SPAN
LANES = 128
CHUNKS = ((0, 80), (80, 80))
WAYS = ((1, slice(0, 256)), (3, slice(256, 512)))


def split_const(table):
    high = table.astype(np.float32).astype(ml_dtypes.bfloat16)
    low = (table - high.astype(np.float64)).astype(np.float32).astype(ml_dtypes.bfloat16)
    return high.astype(np.float32), low.astype(np.float32)


def tables():
    f = np.arange(SPAN, dtype=np.float64)[:, None]
    n = np.arange(SPAN, dtype=np.float64)[None, :]
    c = np.cos(np.pi * (2.0 * n + 1.0) * f / (2.0 * SPAN))
    c = c * np.where(f == 0, np.sqrt(1.0 / SPAN), np.sqrt(2.0 / SPAN))
    c = c[:LOW]
    high, low = split_const(np.kron(np.eye(4), c))
    right = np.zeros((SPAN, OFFSETS, LANES // BAND, BAND))
    right[:] = c.T.reshape(SPAN, OFFSETS, 1, BAND)
    return (
        np.concatenate([high, low], axis=0),
        np.stack([np.ascontiguousarray(high.T), np.ascontiguousarray(low.T)]),
        np.stack(split_const(right.reshape(SPAN, OFFSETS * LANES))),
    )


def dot(a, b, dims=((1,), (0,))):
    return lax.dot_general(a, b, (dims, ((), ())), preferred_element_type=F32)


def split(value):
    high = value.astype(BF)
    return high, (value - high.astype(F32)).astype(BF)


def kernel(
    x_hbm, w_hbm, gain_hbm, cot_hbm, mom_hbm, row_hbm, col_hbm, left_hbm, left_t_hbm, right_hbm,
    upd_v, new_v,
    xv, wv, gain_ref, row_ref, col_ref, momv, left_f, left_t_f, right_f, leftv, left_tv, rightv,
    cot_pair, cot_mix, cot_all, part_out, part_own, part_in, pair, relay, relay_sum, recv, dk, mom_new,
    row_mask, col_mask, band_y, band_xz,
    load_sem, cs_s, cs_r, cz_s, cz_r, ps_s, ps_r, r1_s, r1_r, rd_s, rd_r, r2_s, r2_r, ag_s, ag_r, a2_s, a2_r, fw_s, fw_r,
    y_s, y_r, xz_s, xz_r,
):
    dp = lax.axis_index("dp")
    mp = lax.axis_index("mp")
    zh = mp // 2
    core = mp % 2
    y = dp % NY
    xz = dp // NY
    sib = {"dp": dp, "mp": zh * 2 + (1 - core)}

    def z_peer(step):
        return {"dp": dp, "mp": ((zh + step) % NZ) * 2 + core}

    def y_peer(step):
        return {"dp": xz * NY + (y + step) % NY, "mp": mp}

    def xz_peer(step):
        return {"dp": ((xz + step) % NXZ) * NY + y, "mp": mp}

    barrier = pltpu.get_barrier_semaphore()
    near = [z_peer(s) for s in (2, 1, 3)] + [sib]
    far = [y_peer(s) for s in (4, 3, 5, 2, 6, 1, 7)] + [xz_peer(s) for s in range(1, NXZ)]

    def greet(peers):
        for peer in peers:
            pl.semaphore_signal(barrier, inc=1, device_id=peer, device_id_type=MESH)

    greet(near)
    loads = [pltpu.make_async_copy(w_hbm, wv, load_sem.at[0])]
    for k, (off, rows) in enumerate(CHUNKS):
        at = (slice(None), slice(None), pl.ds(off, rows))
        loads.append(pltpu.make_async_copy(x_hbm.at[at], xv.at[at], load_sem.at[1 + k]))
    base = 1 + len(CHUNKS)
    more = [(cot_hbm, cot_pair.at[core]), (gain_hbm, gain_ref), (row_hbm, row_ref), (col_hbm, col_ref), (mom_hbm, momv)]
    more += [(left_hbm, left_f), (left_t_hbm, left_t_f), (right_hbm, right_f)]
    for k, (src, dst) in enumerate(more):
        loads.append(pltpu.make_async_copy(src, dst, load_sem.at[base + k]))
    for load in loads[: base + 1]:
        load.start()
    greet(far)
    for load in loads[base + 1 :]:
        load.start()

    def remote(src, dst, send, recv_, peer):
        return pltpu.make_async_remote_copy(
            src_ref=src, dst_ref=dst, send_sem=send, recv_sem=recv_, device_id=peer, device_id_type=MESH
        )

    sent = []
    flying = {}

    def start(key, copy):
        copy.start()
        sent.append(copy)
        flying[key] = copy

    def landed(key, copy):
        copy.wait_recv()
        del flying[key]

    part_swaps = []

    def partial_keys(k):
        off, rows = CHUNKS[k]
        loads[1 + k].wait()
        at = pl.ds(off, rows)
        for side, place in ((1 - core, part_out), (core, part_own)):
            x_rows = xv[:, side, at, :].reshape(NZ * rows, WIDTH)
            part = dot(x_rows, wv[...], ((1,), (1,)))
            place[:, at, :] = part.astype(BF).reshape(NZ, rows, KV)

    def swap_parts(k):
        at = (slice(None), pl.ds(*CHUNKS[k]))
        part_swaps.append(remote(part_out.at[at], part_in.at[at], ps_s.at[k], ps_r.at[k], sib))
        start(("ps", k), part_swaps[k])

    loads[0].wait()
    for k in range(len(CHUNKS)):
        partial_keys(k)
    pl.semaphore_wait(barrier, len(near) + len(far))
    for k in range(len(CHUNKS)):
        swap_parts(k)
    cot_swap = remote(cot_hbm, cot_pair.at[core], cs_s, cs_r, sib)
    start(("cs",), cot_swap)

    for k, (off, rows) in enumerate(CHUNKS):
        at = pl.ds(off, rows)
        landed(("ps", k), part_swaps[k])
        pair[:, at, :] = (part_own[:, at, :].astype(F32) + part_in[:, at, :].astype(F32)).astype(BF)
        for way, (step, half) in enumerate(WAYS):
            start(("r1", k, way), remote(
                pair.at[(zh + 2) % NZ, at, half], relay.at[way, at], r1_s.at[k, way], r1_r.at[k, way], z_peer(step)
            ))

    loads[base].wait()
    landed(("cs",), cot_swap)
    cot_mix[...] = cot_pair[...].reshape(LANES, 2 * NZ * OWN).T.reshape(NZ, 2, OWN, LANES)
    cot_all[zh] = cot_mix[zh, core]
    for step in (2, 1, 3):
        start(("cz", step), remote(
            cot_mix.at[(zh + step) % NZ, core], cot_all.at[zh], cz_s.at[step - 1], cz_r.at[step - 1], z_peer(step)
        ))
    for k, (off, rows) in enumerate(CHUNKS):
        at = pl.ds(off, rows)
        for way, (step, half) in enumerate(WAYS):
            other = WAYS[1 - way][1]
            start(("rd", k, way), remote(
                pair.at[(zh + step) % NZ, at, other], recv.at[way, at, other],
                rd_s.at[k, way], rd_r.at[k, way], z_peer(step),
            ))
    for k, (off, rows) in enumerate(CHUNKS):
        at = pl.ds(off, rows)
        for way, (step, half) in enumerate(WAYS):
            landed(("r1", k, way), remote(
                pair.at[0, at, half], relay.at[way, at], r1_s.at[k, way], r1_r.at[k, way], sib
            ))
            both = pair[(zh + step) % NZ, at, half].astype(F32) + relay[way, at, :].astype(F32)
            relay_sum[way, at, :] = both.astype(BF)
            start(("r2", k, way), remote(
                relay_sum.at[way, at], recv.at[way, at, half], r2_s.at[k, way], r2_r.at[k, way], z_peer(step)
            ))

    block_r = lax.broadcasted_iota(jnp.int32, (BAND, WIDTH), 1) // SPAN
    block_c = lax.broadcasted_iota(jnp.int32, (BAND, LANES), 1) // BAND

    def spread(r, carry):
        of_row = jnp.zeros((BAND, WIDTH), jnp.int32)
        of_col = jnp.zeros((BAND, LANES), jnp.int32)
        for c in range(COLS_BLK):
            of_row = jnp.where(block_r == c, row_ref[r, c], of_row)
            of_col = jnp.where(block_c == c, col_ref[r, c], of_col)
        row_mask[r] = of_row
        col_mask[r] = of_col
        return carry

    for load in loads[base + 1 :]:
        load.wait()
    lax.fori_loop(0, ROWS_BLK, spread, 0)
    mom_new[...] = DECAY * momv[0].astype(F32)
    leftv[...] = left_f[...].astype(BF)
    left_tv[...] = left_t_f[...].astype(BF)
    lane_block = (lax.broadcasted_iota(jnp.int32, (SPAN, OFFSETS * LANES), 1) % LANES) // BAND
    for c in range(COLS_BLK):
        for part in range(2):
            rightv[part, c * SPAN : (c + 1) * SPAN] = jnp.where(lane_block == c, right_f[part], 0.0).astype(BF)

    for step in (2, 1, 3):
        src = (zh + NZ - step) % NZ
        landed(("cz", step), remote(cot_mix.at[0, 0], cot_all.at[src], cz_s.at[step - 1], cz_r.at[step - 1], sib))
    gain = gain_ref[...]
    for k, (off, rows) in enumerate(CHUNKS):
        at = pl.ds(off, rows)
        for way, (step, half) in enumerate(WAYS):
            other = WAYS[1 - way][1]
            landed(("rd", k, way), remote(
                pair.at[0, at, other], recv.at[way, at, other], rd_s.at[k, way], rd_r.at[k, way], sib
            ))
        for way, (step, half) in enumerate(WAYS):
            landed(("r2", k, way), remote(
                relay_sum.at[way, at], recv.at[way, at, half], r2_s.at[k, way], r2_r.at[k, way], sib
            ))
        keys = pair[zh, at, :].astype(F32) + recv[0, at, :].astype(F32) + recv[1, at, :].astype(F32)
        scaled = gain * jnp.concatenate([cot_all[j, at, :].astype(F32) for j in range(NZ)], axis=-1)
        inverse = lax.rsqrt(jnp.mean(keys * keys, axis=-1, keepdims=True) + EPS)
        inner = jnp.sum(scaled * keys, axis=-1, keepdims=True)
        dk[mp, at, :] = (inverse * scaled - (inverse * inverse * inverse * inner / KV) * keys).astype(BF)
        mine = dk.at[mp, at]
        for way, (step, half) in enumerate(WAYS):
            start(("ag", k, way), remote(mine, mine, ag_s.at[k, way], ag_r.at[k, way], z_peer(step)))
        start(("fw", k, 0), remote(mine, mine, fw_s.at[k, 0], fw_r.at[k, 0], sib))

    def owner(step, side):
        return ((zh + NZ - step) % NZ) * 2 + side

    for k, (off, rows) in enumerate(CHUNKS):
        at = pl.ds(off, rows)
        for way, (step, half) in enumerate(WAYS):
            got = dk.at[owner(step, core), at]
            landed(("ag", k, way), remote(got, got, ag_s.at[k, way], ag_r.at[k, way], sib))
            part = dk.at[owner(step, core), at, half]
            start(("a2", k, way), remote(part, part, a2_s.at[k, way], a2_r.at[k, way], z_peer(step)))
            start(("fw", k, step), remote(got, got, fw_s.at[k, step], fw_r.at[k, step], sib))
    for k, (off, rows) in enumerate(CHUNKS):
        at = pl.ds(off, rows)
        for way, (step, half) in enumerate(WAYS):
            part = dk.at[owner(2, core), at, half]
            landed(("a2", k, way), remote(part, part, a2_s.at[k, way], a2_r.at[k, way], sib))
        got = dk.at[owner(2, core), at]
        start(("fw", k, 2), remote(got, got, fw_s.at[k, 2], fw_r.at[k, 2], sib))
        for step in (0, 1, 3, 2):
            got = dk.at[owner(step, 1 - core), at]
            landed(("fw", k, step), remote(got, got, fw_s.at[k, step], fw_r.at[k, step], sib))
        all_dk = dk[:, at, :].reshape(2 * NZ * rows, KV)
        all_x = xv[:, :, at, :].reshape(2 * NZ * rows, WIDTH)
        mom_new[...] += dot(all_dk, all_x, ((0,), (0,))) * (1.0 / math.sqrt(2 * NZ * OWN))

    picked = []
    for g in range(2):
        high, low = split(mom_new[g * 256 : (g + 1) * 256, :])
        both = dot(leftv[...], high)
        sect = both[:128] + both[128:] + dot(leftv[:128], low)
        sect = sect.reshape(4, OFFSETS, BAND, WIDTH)
        chosen = row_mask[g * 4 : (g + 1) * 4]
        total = jnp.zeros((4, BAND, WIDTH), F32)
        for band in range(OFFSETS):
            total = total + jnp.where(chosen == band, sect[:, band], 0.0)
        picked.append(total.reshape(32, WIDTH))
    sect = jnp.concatenate(picked, axis=0)
    high, low = split(sect)
    both = dot(jnp.concatenate([high, low], axis=0), rightv[0])
    full = both[:64] + both[64:] + dot(high, rightv[1])
    chosen = col_mask[...].reshape(64, LANES)
    coeffs = jnp.zeros((64, LANES), F32)
    for band in range(OFFSETS):
        coeffs = coeffs + jnp.where(chosen == band, full[:, band * LANES : (band + 1) * LANES], 0.0)

    band_y[y] = coeffs.astype(BF)
    for step in (4, 3, 5, 2, 6, 1, 7):
        start(("y", step), remote(band_y.at[y], band_y.at[y], y_s.at[step - 1], y_r.at[step - 1], y_peer(step)))

    def rebuild(values, exact, put):
        parts = [jnp.where(chosen == band, values, 0.0) for band in range(OFFSETS)]
        high, low = split(jnp.concatenate(parts, axis=1))
        if exact:
            both = dot(jnp.concatenate([high, low], axis=0), rightv[0], ((1,), (1,)))
            first = both[:64] + both[64:] + dot(high, rightv[1], ((1,), (1,)))
        else:
            first = dot(high, rightv[0], ((1,), (1,)))
        for g in range(2):
            rows = first[g * 32 : (g + 1) * 32].reshape(4, 1, BAND, WIDTH)
            bands = lax.broadcasted_iota(jnp.int32, (4, OFFSETS, BAND, WIDTH), 1)
            mask = row_mask[g * 4 : (g + 1) * 4].reshape(4, 1, BAND, WIDTH)
            spread_rows = jnp.where(mask == bands, rows, 0.0).reshape(128, WIDTH)
            high, low = split(spread_rows)
            out = dot(left_tv[0], high)
            if exact:
                out = out + dot(left_tv[1], high) + dot(left_tv[0], low)
            put(g, out)

    def put_new(g, own):
        at = slice(g * 256, (g + 1) * 256)
        new_v[0, at, :] = (mom_new[at, :] - own).astype(BF)

    rebuild(coeffs, True, put_new)

    for step in (1, 7, 2, 6, 3, 5, 4):
        got = band_y.at[(y + NY - step) % NY]
        landed(("y", step), remote(got, got, y_s.at[step - 1], y_r.at[step - 1], sib))
    total = band_y[0].astype(F32)
    for j in range(1, NY):
        total = total + band_y[j].astype(F32)
    band_xz[xz] = total.astype(BF)
    for step in range(1, NXZ):
        start(("xz", step), remote(band_xz.at[xz], band_xz.at[xz], xz_s.at[step - 1], xz_r.at[step - 1], xz_peer(step)))
    for step in range(1, NXZ):
        got = band_xz.at[(xz + NXZ - step) % NXZ]
        landed(("xz", step), remote(got, got, xz_s.at[step - 1], xz_r.at[step - 1], sib))
    total = band_xz[0].astype(F32)
    for j in range(1, NXZ):
        total = total + band_xz[j].astype(F32)

    def put_update(g, value):
        upd_v[g * 256 : (g + 1) * 256, :] = value.astype(BF)

    rebuild(total * (1.0 / N_DP), False, put_update)
    for copy in sent:
        copy.wait_send()


def hbm(value):
    return pltpu.with_memory_space_constraint(value, pltpu.HBM)


def on_device(tokens, key_weight, key_gain, cotangent, momentum, band_row, band_col):
    left, left_t, right = tables()
    n = len(CHUNKS)
    any_spec = pl.BlockSpec(memory_space=pltpu.HBM)
    vmem = pl.BlockSpec(memory_space=pltpu.VMEM)
    dma = pltpu.SemaphoreType.DMA
    return pl.pallas_call(
        kernel,
        out_shape=(
            jax.ShapeDtypeStruct((KV, WIDTH), BF),
            jax.ShapeDtypeStruct((1, KV, WIDTH), BF),
        ),
        in_specs=[any_spec] * 10,
        out_specs=(vmem, vmem),
        scratch_shapes=[
            pltpu.VMEM((NZ, 2, OWN, WIDTH), BF),
            pltpu.VMEM((KV, WIDTH), BF),
            pltpu.VMEM((1, KV), F32),
            pltpu.SMEM((ROWS_BLK, COLS_BLK), jnp.int32),
            pltpu.SMEM((ROWS_BLK, COLS_BLK), jnp.int32),
            pltpu.VMEM((1, KV, WIDTH), BF),
            pltpu.VMEM(left.shape, F32),
            pltpu.VMEM(left_t.shape, F32),
            pltpu.VMEM(right.shape, F32),
            pltpu.VMEM(left.shape, BF),
            pltpu.VMEM(left_t.shape, BF),
            pltpu.VMEM((2, WIDTH, OFFSETS * LANES), BF),
            pltpu.VMEM((2, SPAN, 2 * NZ * OWN), BF),
            pltpu.VMEM((NZ, 2, OWN, LANES), BF),
            pltpu.VMEM((NZ, OWN, LANES), BF),
            pltpu.VMEM((NZ, OWN, KV), BF),
            pltpu.VMEM((NZ, OWN, KV), BF),
            pltpu.VMEM((NZ, OWN, KV), BF),
            pltpu.VMEM((NZ, OWN, KV), BF),
            pltpu.VMEM((2, OWN, KV // 2), BF),
            pltpu.VMEM((2, OWN, KV // 2), BF),
            pltpu.VMEM((2, OWN, KV), BF),
            pltpu.VMEM((2 * NZ, OWN, KV), BF),
            pltpu.VMEM((KV, WIDTH), F32),
            pltpu.VMEM((ROWS_BLK, BAND, WIDTH), jnp.int32),
            pltpu.VMEM((ROWS_BLK, BAND, LANES), jnp.int32),
            pltpu.VMEM((NY, 64, LANES), BF),
            pltpu.VMEM((NXZ, 64, LANES), BF),
            dma((9 + n,)),
            dma(()),
            dma(()),
            dma((3,)),
            dma((3,)),
            dma((n,)),
            dma((n,)),
            dma((n, 2)),
            dma((n, 2)),
            dma((n, 2)),
            dma((n, 2)),
            dma((n, 2)),
            dma((n, 2)),
            dma((n, 2)),
            dma((n, 2)),
            dma((n, 2)),
            dma((n, 2)),
            dma((n, 4)),
            dma((n, 4)),
            dma((7,)),
            dma((7,)),
            dma((7,)),
            dma((7,)),
        ],
        compiler_params=pltpu.CompilerParams(
            collective_id=0, has_side_effects=True, vmem_limit_bytes=48 * 1024 * 1024
        ),
        cost_estimate=pl.CostEstimate(flops=2_500_000_000, bytes_accessed=6_000_000, transcendentals=1280),
    )(
        hbm(tokens.reshape(NZ, 2, OWN, WIDTH)),
        hbm(key_weight),
        hbm(key_gain.reshape(1, KV)),
        hbm(cotangent.T),
        hbm(momentum),
        hbm(band_row),
        hbm(band_col),
        hbm(left),
        hbm(left_t),
        hbm(right),
    )


def solution(mesh):
    return jax.shard_map(
        on_device,
        mesh=mesh,
        in_specs=(
            P("dp", "mp"),
            P(None, "mp"),
            P(),
            P("dp", "mp"),
            P("dp", None, "mp"),
            P(None, "mp"),
            P(None, "mp"),
        ),
        out_specs=(P(None, "mp"), P("dp", None, "mp")),
        check_vma=False,
    )
```

```python
import math

import jax
import jax.numpy as jnp
import ml_dtypes
import numpy as np
from jax import lax
from jax.experimental import pallas as pl
from jax.experimental.pallas import tpu as pltpu
from jax.sharding import PartitionSpec as P

MESH = pl.DeviceIdType.MESH
BF = jnp.bfloat16
F32 = jnp.float32

SPAN = 64
BAND = 8
OFFSETS = 4
LOW = BAND * OFFSETS
EPS = 1e-06
DECAY = 0.9

NY = 8
NXZ = 8
NZ = 4
N_DP = NY * NXZ
OWN = 160
KV = 512
WIDTH = 640
ROWS_BLK = KV // SPAN
COLS_BLK = WIDTH // SPAN
LANES = 128
WINDOW = 3 * LANES
CHUNKS = ((0, 80), (80, 80))
WAYS = ((1, slice(0, 256)), (3, slice(256, 512)))


def split_const(table):
    high = table.astype(np.float32).astype(ml_dtypes.bfloat16)
    low = (table - high.astype(np.float64)).astype(np.float32).astype(ml_dtypes.bfloat16)
    return high.astype(np.float32), low.astype(np.float32)


def tables():
    f = np.arange(SPAN, dtype=np.float64)[:, None]
    n = np.arange(SPAN, dtype=np.float64)[None, :]
    c = np.cos(np.pi * (2.0 * n + 1.0) * f / (2.0 * SPAN))
    c = c * np.where(f == 0, np.sqrt(1.0 / SPAN), np.sqrt(2.0 / SPAN))
    c = c[:LOW]
    high, low = split_const(np.kron(np.eye(4), c))
    right = np.zeros((SPAN, OFFSETS, LANES // BAND, BAND))
    right[:] = c.T.reshape(SPAN, OFFSETS, 1, BAND)
    return (
        np.concatenate([high, low], axis=0),
        np.stack([np.ascontiguousarray(high.T), np.ascontiguousarray(low.T)]),
        np.stack(split_const(right.reshape(SPAN, OFFSETS * LANES))),
    )


def dot(a, b, dims=((1,), (0,))):
    return lax.dot_general(a, b, (dims, ((), ())), preferred_element_type=F32)


def split(value):
    high = value.astype(BF)
    return high, (value - high.astype(F32)).astype(BF)


def kernel(
    x_hbm, w_hbm, gain_hbm, cot_hbm, mom_hbm, row_hbm, col_hbm, left_hbm, left_t_hbm, right_hbm,
    upd_v, new_v,
    xv, wv, gain_ref, row_ref, col_ref, momv, left_f, left_t_f, right_f, leftv, left_tv, rightv,
    cot_in, cot_t, part_out, part_own, part_in, pair, relay, relay_sum, recv, dk, mom_new,
    row_mask, col_mask, band_y, band_xz,
    load_sem, cs_s, cs_r, cz_s, cz_r, ps_s, ps_r, r1_s, r1_r, rd_s, rd_r, r2_s, r2_r, ag_s, ag_r, a2_s, a2_r, fw_s, fw_r,
    y_s, y_r, xz_s, xz_r,
):
    dp = lax.axis_index("dp")
    mp = lax.axis_index("mp")
    zh = mp // 2
    core = mp % 2
    y = dp % NY
    xz = dp // NY
    sib = {"dp": dp, "mp": zh * 2 + (1 - core)}

    def z_peer(step):
        return {"dp": dp, "mp": ((zh + step) % NZ) * 2 + core}

    def y_peer(step):
        return {"dp": xz * NY + (y + step) % NY, "mp": mp}

    def xz_peer(step):
        return {"dp": ((xz + step) % NXZ) * NY + y, "mp": mp}

    barrier = pltpu.get_barrier_semaphore()
    near = [z_peer(s) for s in (2, 1, 3)] + [sib]
    far = [y_peer(s) for s in (4, 3, 5, 2, 6, 1, 7)] + [xz_peer(s) for s in range(1, NXZ)]

    def greet(peers):
        for peer in peers:
            pl.semaphore_signal(barrier, inc=1, device_id=peer, device_id_type=MESH)

    greet(near)
    loads = [pltpu.make_async_copy(w_hbm, wv, load_sem.at[0])]
    for k, (off, rows) in enumerate(CHUNKS):
        at = (slice(None), slice(None), pl.ds(off, rows))
        loads.append(pltpu.make_async_copy(x_hbm.at[at], xv.at[at], load_sem.at[1 + k]))
    base = 1 + len(CHUNKS)
    more = [(cot_hbm.at[:, pl.ds(pl.multiple_of((zh * 5 // 2) * LANES, LANES), WINDOW)], cot_in.at[zh, core]), (gain_hbm, gain_ref), (row_hbm, row_ref), (col_hbm, col_ref), (mom_hbm, momv)]
    more += [(left_hbm, left_f), (left_t_hbm, left_t_f), (right_hbm, right_f)]
    for k, (src, dst) in enumerate(more):
        loads.append(pltpu.make_async_copy(src, dst, load_sem.at[base + k]))
    for load in loads[: base + 1]:
        load.start()
    greet(far)
    for load in loads[base + 1 :]:
        load.start()

    def window(chip):
        return pl.ds(pl.multiple_of((chip * 5 // 2) * LANES, LANES), WINDOW)

    def remote(src, dst, send, recv_, peer):
        return pltpu.make_async_remote_copy(
            src_ref=src, dst_ref=dst, send_sem=send, recv_sem=recv_, device_id=peer, device_id_type=MESH
        )

    sent = []
    flying = {}

    def start(key, copy):
        copy.start()
        sent.append(copy)
        flying[key] = copy

    def landed(key, copy):
        copy.wait_recv()
        del flying[key]

    part_swaps = []

    def partial_keys(k):
        off, rows = CHUNKS[k]
        loads[1 + k].wait()
        at = pl.ds(off, rows)
        for side, place in ((1 - core, part_out), (core, part_own)):
            x_rows = xv[:, side, at, :].reshape(NZ * rows, WIDTH)
            part = dot(x_rows, wv[...], ((1,), (1,)))
            place[:, at, :] = part.astype(BF).reshape(NZ, rows, KV)

    def swap_parts(k):
        at = (slice(None), pl.ds(*CHUNKS[k]))
        part_swaps.append(remote(part_out.at[at], part_in.at[at], ps_s.at[k], ps_r.at[k], sib))
        start(("ps", k), part_swaps[k])

    loads[0].wait()
    for k in range(len(CHUNKS)):
        partial_keys(k)
    pl.semaphore_wait(barrier, len(near) + len(far))
    for step in (2, 1, 3):
        start(("cz", step), remote(
            cot_hbm.at[:, window((zh + step) % NZ)], cot_in.at[zh, core],
            cz_s.at[step - 1], cz_r.at[step - 1], z_peer(step),
        ))
    for k in range(len(CHUNKS)):
        swap_parts(k)
    for k, (off, rows) in enumerate(CHUNKS):
        at = pl.ds(off, rows)
        landed(("ps", k), part_swaps[k])
        pair[:, at, :] = (part_own[:, at, :].astype(F32) + part_in[:, at, :].astype(F32)).astype(BF)
        for way, (step, half) in enumerate(WAYS):
            start(("r1", k, way), remote(
                pair.at[(zh + 2) % NZ, at, half], relay.at[way, at], r1_s.at[k, way], r1_r.at[k, way], z_peer(step)
            ))

    for k, (off, rows) in enumerate(CHUNKS):
        at = pl.ds(off, rows)
        for way, (step, half) in enumerate(WAYS):
            other = WAYS[1 - way][1]
            start(("rd", k, way), remote(
                pair.at[(zh + step) % NZ, at, other], recv.at[way, at, other],
                rd_s.at[k, way], rd_r.at[k, way], z_peer(step),
            ))
    for k, (off, rows) in enumerate(CHUNKS):
        at = pl.ds(off, rows)
        for way, (step, half) in enumerate(WAYS):
            landed(("r1", k, way), remote(
                pair.at[0, at, half], relay.at[way, at], r1_s.at[k, way], r1_r.at[k, way], sib
            ))
            both = pair[(zh + step) % NZ, at, half].astype(F32) + relay[way, at, :].astype(F32)
            relay_sum[way, at, :] = both.astype(BF)
            start(("r2", k, way), remote(
                relay_sum.at[way, at], recv.at[way, at, half], r2_s.at[k, way], r2_r.at[k, way], z_peer(step)
            ))

    block_r = lax.broadcasted_iota(jnp.int32, (BAND, WIDTH), 1) // SPAN
    block_c = lax.broadcasted_iota(jnp.int32, (BAND, LANES), 1) // BAND

    def spread(r, carry):
        of_row = jnp.zeros((BAND, WIDTH), jnp.int32)
        of_col = jnp.zeros((BAND, LANES), jnp.int32)
        for c in range(COLS_BLK):
            of_row = jnp.where(block_r == c, row_ref[r, c], of_row)
            of_col = jnp.where(block_c == c, col_ref[r, c], of_col)
        row_mask[r] = of_row
        col_mask[r] = of_col
        return carry

    for load in loads[base + 1 :]:
        load.wait()
    lax.fori_loop(0, ROWS_BLK, spread, 0)
    mom_new[...] = DECAY * momv[0].astype(F32)
    leftv[...] = left_f[...].astype(BF)
    left_tv[...] = left_t_f[...].astype(BF)
    lane_block = (lax.broadcasted_iota(jnp.int32, (SPAN, OFFSETS * LANES), 1) % LANES) // BAND
    for c in range(COLS_BLK):
        for part in range(2):
            rightv[part, c * SPAN : (c + 1) * SPAN] = jnp.where(lane_block == c, right_f[part], 0.0).astype(BF)

    loads[base].wait()
    for step in (1, 3, 2):
        src = (zh + NZ - step) % NZ
        landed(("cz", step), remote(
            cot_hbm.at[:, pl.ds(0, WINDOW)], cot_in.at[src, core], cz_s.at[step - 1], cz_r.at[step - 1], sib
        ))
    start(("cs",), remote(cot_in.at[:, core], cot_in.at[:, core], cs_s, cs_r, sib))
    landed(("cs",), remote(cot_in.at[:, 1 - core], cot_in.at[:, 1 - core], cs_s, cs_r, sib))
    cot_t[...] = cot_in[...].reshape(KV, WINDOW).T.astype(F32)
    cot_base = pl.multiple_of((zh % 2) * 64 + core * OWN, 32)
    gain = gain_ref[...]
    for k, (off, rows) in enumerate(CHUNKS):
        at = pl.ds(off, rows)
        for way, (step, half) in enumerate(WAYS):
            other = WAYS[1 - way][1]
            landed(("rd", k, way), remote(
                pair.at[0, at, other], recv.at[way, at, other], rd_s.at[k, way], rd_r.at[k, way], sib
            ))
        for way, (step, half) in enumerate(WAYS):
            landed(("r2", k, way), remote(
                relay_sum.at[way, at], recv.at[way, at, half], r2_s.at[k, way], r2_r.at[k, way], sib
            ))
        keys = pair[zh, at, :].astype(F32) + recv[0, at, :].astype(F32) + recv[1, at, :].astype(F32)
        scaled = gain * cot_t[pl.ds(cot_base + off, rows), :]
        inverse = lax.rsqrt(jnp.mean(keys * keys, axis=-1, keepdims=True) + EPS)
        inner = jnp.sum(scaled * keys, axis=-1, keepdims=True)
        dk[mp, at, :] = (inverse * scaled - (inverse * inverse * inverse * inner / KV) * keys).astype(BF)
        mine = dk.at[mp, at]
        for way, (step, half) in enumerate(WAYS):
            start(("ag", k, way), remote(mine, mine, ag_s.at[k, way], ag_r.at[k, way], z_peer(step)))
        start(("fw", k, 0), remote(mine, mine, fw_s.at[k, 0], fw_r.at[k, 0], sib))

    def owner(step, side):
        return ((zh + NZ - step) % NZ) * 2 + side

    for k, (off, rows) in enumerate(CHUNKS):
        at = pl.ds(off, rows)
        for way, (step, half) in enumerate(WAYS):
            got = dk.at[owner(step, core), at]
            landed(("ag", k, way), remote(got, got, ag_s.at[k, way], ag_r.at[k, way], sib))
            part = dk.at[owner(step, core), at, half]
            start(("a2", k, way), remote(part, part, a2_s.at[k, way], a2_r.at[k, way], z_peer(step)))
            start(("fw", k, step), remote(got, got, fw_s.at[k, step], fw_r.at[k, step], sib))
    for k, (off, rows) in enumerate(CHUNKS):
        at = pl.ds(off, rows)
        for way, (step, half) in enumerate(WAYS):
            part = dk.at[owner(2, core), at, half]
            landed(("a2", k, way), remote(part, part, a2_s.at[k, way], a2_r.at[k, way], sib))
        got = dk.at[owner(2, core), at]
        start(("fw", k, 2), remote(got, got, fw_s.at[k, 2], fw_r.at[k, 2], sib))
        for step in (0, 1, 3, 2):
            got = dk.at[owner(step, 1 - core), at]
            landed(("fw", k, step), remote(got, got, fw_s.at[k, step], fw_r.at[k, step], sib))
        all_dk = dk[:, at, :].reshape(2 * NZ * rows, KV)
        all_x = xv[:, :, at, :].reshape(2 * NZ * rows, WIDTH)
        mom_new[...] += dot(all_dk, all_x, ((0,), (0,))) * (1.0 / math.sqrt(2 * NZ * OWN))

    picked = []
    for g in range(2):
        high, low = split(mom_new[g * 256 : (g + 1) * 256, :])
        both = dot(leftv[...], high)
        sect = both[:128] + both[128:] + dot(leftv[:128], low)
        sect = sect.reshape(4, OFFSETS, BAND, WIDTH)
        chosen = row_mask[g * 4 : (g + 1) * 4]
        total = jnp.zeros((4, BAND, WIDTH), F32)
        for band in range(OFFSETS):
            total = total + jnp.where(chosen == band, sect[:, band], 0.0)
        picked.append(total.reshape(32, WIDTH))
    sect = jnp.concatenate(picked, axis=0)
    high, low = split(sect)
    both = dot(jnp.concatenate([high, low], axis=0), rightv[0])
    full = both[:64] + both[64:] + dot(high, rightv[1])
    chosen = col_mask[...].reshape(64, LANES)
    coeffs = jnp.zeros((64, LANES), F32)
    for band in range(OFFSETS):
        coeffs = coeffs + jnp.where(chosen == band, full[:, band * LANES : (band + 1) * LANES], 0.0)

    band_y[y] = coeffs.astype(BF)
    for step in (4, 3, 5, 2, 6, 1, 7):
        start(("y", step), remote(band_y.at[y], band_y.at[y], y_s.at[step - 1], y_r.at[step - 1], y_peer(step)))

    def rebuild(values, exact, put):
        parts = [jnp.where(chosen == band, values, 0.0) for band in range(OFFSETS)]
        high, low = split(jnp.concatenate(parts, axis=1))
        if exact:
            both = dot(jnp.concatenate([high, low], axis=0), rightv[0], ((1,), (1,)))
            first = both[:64] + both[64:] + dot(high, rightv[1], ((1,), (1,)))
        else:
            first = dot(high, rightv[0], ((1,), (1,)))
        for g in range(2):
            rows = first[g * 32 : (g + 1) * 32].reshape(4, 1, BAND, WIDTH)
            bands = lax.broadcasted_iota(jnp.int32, (4, OFFSETS, BAND, WIDTH), 1)
            mask = row_mask[g * 4 : (g + 1) * 4].reshape(4, 1, BAND, WIDTH)
            spread_rows = jnp.where(mask == bands, rows, 0.0).reshape(128, WIDTH)
            high, low = split(spread_rows)
            out = dot(left_tv[0], high)
            if exact:
                out = out + dot(left_tv[1], high) + dot(left_tv[0], low)
            put(g, out)

    def put_new(g, own):
        at = slice(g * 256, (g + 1) * 256)
        new_v[0, at, :] = (mom_new[at, :] - own).astype(BF)

    rebuild(coeffs, True, put_new)

    for step in (1, 7, 2, 6, 3, 5, 4):
        got = band_y.at[(y + NY - step) % NY]
        landed(("y", step), remote(got, got, y_s.at[step - 1], y_r.at[step - 1], sib))
    total = band_y[0].astype(F32)
    for j in range(1, NY):
        total = total + band_y[j].astype(F32)
    band_xz[xz] = total.astype(BF)
    for step in range(1, NXZ):
        start(("xz", step), remote(band_xz.at[xz], band_xz.at[xz], xz_s.at[step - 1], xz_r.at[step - 1], xz_peer(step)))
    for step in range(1, NXZ):
        got = band_xz.at[(xz + NXZ - step) % NXZ]
        landed(("xz", step), remote(got, got, xz_s.at[step - 1], xz_r.at[step - 1], sib))
    total = band_xz[0].astype(F32)
    for j in range(1, NXZ):
        total = total + band_xz[j].astype(F32)

    def put_update(g, value):
        upd_v[g * 256 : (g + 1) * 256, :] = value.astype(BF)

    rebuild(total * (1.0 / N_DP), False, put_update)
    for copy in sent:
        copy.wait_send()


def hbm(value):
    return pltpu.with_memory_space_constraint(value, pltpu.HBM)


def on_device(tokens, key_weight, key_gain, cotangent, momentum, band_row, band_col):
    left, left_t, right = tables()
    n = len(CHUNKS)
    any_spec = pl.BlockSpec(memory_space=pltpu.HBM)
    vmem = pl.BlockSpec(memory_space=pltpu.VMEM)
    dma = pltpu.SemaphoreType.DMA
    return pl.pallas_call(
        kernel,
        out_shape=(
            jax.ShapeDtypeStruct((KV, WIDTH), BF),
            jax.ShapeDtypeStruct((1, KV, WIDTH), BF),
        ),
        in_specs=[any_spec] * 10,
        out_specs=(vmem, vmem),
        scratch_shapes=[
            pltpu.VMEM((NZ, 2, OWN, WIDTH), BF),
            pltpu.VMEM((KV, WIDTH), BF),
            pltpu.VMEM((1, KV), F32),
            pltpu.SMEM((ROWS_BLK, COLS_BLK), jnp.int32),
            pltpu.SMEM((ROWS_BLK, COLS_BLK), jnp.int32),
            pltpu.VMEM((1, KV, WIDTH), BF),
            pltpu.VMEM(left.shape, F32),
            pltpu.VMEM(left_t.shape, F32),
            pltpu.VMEM(right.shape, F32),
            pltpu.VMEM(left.shape, BF),
            pltpu.VMEM(left_t.shape, BF),
            pltpu.VMEM((2, WIDTH, OFFSETS * LANES), BF),
            pltpu.VMEM((NZ, 2, KV // (2 * NZ), WINDOW), BF),
            pltpu.VMEM((WINDOW, KV), F32),
            pltpu.VMEM((NZ, OWN, KV), BF),
            pltpu.VMEM((NZ, OWN, KV), BF),
            pltpu.VMEM((NZ, OWN, KV), BF),
            pltpu.VMEM((NZ, OWN, KV), BF),
            pltpu.VMEM((2, OWN, KV // 2), BF),
            pltpu.VMEM((2, OWN, KV // 2), BF),
            pltpu.VMEM((2, OWN, KV), BF),
            pltpu.VMEM((2 * NZ, OWN, KV), BF),
            pltpu.VMEM((KV, WIDTH), F32),
            pltpu.VMEM((ROWS_BLK, BAND, WIDTH), jnp.int32),
            pltpu.VMEM((ROWS_BLK, BAND, LANES), jnp.int32),
            pltpu.VMEM((NY, 64, LANES), BF),
            pltpu.VMEM((NXZ, 64, LANES), BF),
            dma((9 + n,)),
            dma(()),
            dma(()),
            dma((3,)),
            dma((3,)),
            dma((n,)),
            dma((n,)),
            dma((n, 2)),
            dma((n, 2)),
            dma((n, 2)),
            dma((n, 2)),
            dma((n, 2)),
            dma((n, 2)),
            dma((n, 2)),
            dma((n, 2)),
            dma((n, 2)),
            dma((n, 2)),
            dma((n, 4)),
            dma((n, 4)),
            dma((7,)),
            dma((7,)),
            dma((7,)),
            dma((7,)),
        ],
        compiler_params=pltpu.CompilerParams(
            collective_id=0, has_side_effects=True, vmem_limit_bytes=48 * 1024 * 1024
        ),
        cost_estimate=pl.CostEstimate(flops=2_500_000_000, bytes_accessed=6_000_000, transcendentals=1280),
    )(
        hbm(tokens.reshape(NZ, 2, OWN, WIDTH)),
        hbm(key_weight),
        hbm(key_gain.reshape(1, KV)),
        hbm(cotangent.T),
        hbm(momentum),
        hbm(band_row),
        hbm(band_col),
        hbm(left),
        hbm(left_t),
        hbm(right),
    )


def solution(mesh):
    return jax.shard_map(
        on_device,
        mesh=mesh,
        in_specs=(
            P("dp", "mp"),
            P(None, "mp"),
            P(),
            P("dp", "mp"),
            P("dp", None, "mp"),
            P(None, "mp"),
            P(None, "mp"),
        ),
        out_specs=(P(None, "mp"), P("dp", None, "mp")),
        check_vma=False,
    )
```

```python
import math

import jax
import jax.numpy as jnp
import ml_dtypes
import numpy as np
from jax import lax
from jax.experimental import pallas as pl
from jax.experimental.pallas import tpu as pltpu
from jax.sharding import PartitionSpec as P

MESH = pl.DeviceIdType.MESH
BF = jnp.bfloat16
F32 = jnp.float32

SPAN = 64
BAND = 8
OFFSETS = 4
LOW = BAND * OFFSETS
EPS = 1e-06
DECAY = 0.9

NY = 8
NXZ = 8
NZ = 4
N_DP = NY * NXZ
OWN = 160
KV = 512
WIDTH = 640
ROWS_BLK = KV // SPAN
COLS_BLK = WIDTH // SPAN
LANES = 128
WINDOW = 3 * LANES
CHUNKS = ((0, 64), (64, 96))
FEATURES = (slice(0, 32), slice(32, 64))
WAYS = ((1, slice(0, 256)), (3, slice(256, 512)))


def split_const(table):
    high = table.astype(np.float32).astype(ml_dtypes.bfloat16)
    low = (table - high.astype(np.float64)).astype(np.float32).astype(ml_dtypes.bfloat16)
    return high.astype(np.float32), low.astype(np.float32)


def tables():
    f = np.arange(SPAN, dtype=np.float64)[:, None]
    n = np.arange(SPAN, dtype=np.float64)[None, :]
    c = np.cos(np.pi * (2.0 * n + 1.0) * f / (2.0 * SPAN))
    c = c * np.where(f == 0, np.sqrt(1.0 / SPAN), np.sqrt(2.0 / SPAN))
    c = c[:LOW]
    high, low = split_const(np.kron(np.eye(4), c))
    right = np.zeros((SPAN, OFFSETS, LANES // BAND, BAND))
    right[:] = c.T.reshape(SPAN, OFFSETS, 1, BAND)
    return (
        np.concatenate([high, low], axis=0),
        np.stack([np.ascontiguousarray(high.T), np.ascontiguousarray(low.T)]),
        np.stack(split_const(right.reshape(SPAN, OFFSETS * LANES))),
    )


def dot(a, b, dims=((1,), (0,))):
    return lax.dot_general(a, b, (dims, ((), ())), preferred_element_type=F32)


def split(value):
    high = value.astype(BF)
    return high, (value - high.astype(F32)).astype(BF)


def kernel(
    x_hbm, w_hbm, gain_hbm, cot_hbm, mom_hbm, row_hbm, col_hbm, left_hbm, left_t_hbm, right_hbm,
    upd_v, new_v,
    xv, wv, gain_ref, row_ref, col_ref, momv, left_f, left_t_f, right_f, leftv, left_tv, rightv,
    cot_in, cot_relay, cot_t, part_out, part_own, part_in, pair, relay, relay_sum, recv, dk, mom_new, sections,
    row_mask, col_mask, band_y, band_xz,
    load_sem, cs_s, cs_r, cr_s, cr_r, cf_s, cf_r, cz_s, cz_r, ps_s, ps_r, r1_s, r1_r, rd_s, rd_r, r2_s, r2_r, ag_s, ag_r, a2_s, a2_r, fw_s, fw_r,
    y_s, y_r, xz_s, xz_r, heard,
):
    dp = lax.axis_index("dp")
    mp = lax.axis_index("mp")
    zh = mp // 2
    core = mp % 2
    y = dp % NY
    xz = dp // NY
    sib = {"dp": dp, "mp": zh * 2 + (1 - core)}

    def z_peer(step):
        return {"dp": dp, "mp": ((zh + step) % NZ) * 2 + core}

    def y_peer(step):
        return {"dp": xz * NY + (y + step) % NY, "mp": mp}

    def xz_peer(step):
        return {"dp": ((xz + step) % NXZ) * NY + y, "mp": mp}

    barrier = pltpu.get_barrier_semaphore()
    def x_peer(step, flip):
        return {"dp": (((xz // 2 + step) % (NXZ // 2)) * 2 + (xz % 2 + flip) % 2) * NY + y, "mp": mp}

    near = [z_peer(1), z_peer(3), sib]
    far = [y_peer(s) for s in (2, 6, 1, 7)]
    far += [x_peer(2, 0), x_peer(1, 1), x_peer(3, 1), x_peer(1, 0), x_peer(3, 0), x_peer(0, 1)]

    def greet(peers):
        for peer in peers:
            pl.semaphore_signal(barrier, inc=1, device_id=peer, device_id_type=MESH)

    greet(near)
    loads = [pltpu.make_async_copy(w_hbm, wv, load_sem.at[0])]
    for k, (off, rows) in enumerate(CHUNKS):
        at = (slice(None), slice(None), pl.ds(off, rows))
        loads.append(pltpu.make_async_copy(x_hbm.at[at], xv.at[at], load_sem.at[1 + k]))
    base = 1 + len(CHUNKS)
    more = [(cot_hbm.at[:, pl.ds(pl.multiple_of((zh * 5 // 2) * LANES, LANES), WINDOW)], cot_in.at[zh, core]), (gain_hbm, gain_ref), (row_hbm, row_ref), (col_hbm, col_ref), (mom_hbm, momv)]
    more += [(left_hbm, left_f), (left_t_hbm, left_t_f), (right_hbm, right_f)]
    for k, (src, dst) in enumerate(more):
        loads.append(pltpu.make_async_copy(src, dst, load_sem.at[base + k]))
    for load in loads[: base + 1]:
        load.start()
    greet(far)
    for load in loads[base + 1 :]:
        load.start()

    def window(chip):
        return pl.ds(pl.multiple_of((chip * 5 // 2) * LANES, LANES), WINDOW)

    def remote(src, dst, send, recv_, peer):
        return pltpu.make_async_remote_copy(
            src_ref=src, dst_ref=dst, send_sem=send, recv_sem=recv_, device_id=peer, device_id_type=MESH
        )

    sent = []
    flying = {}

    def start(key, copy):
        copy.start()
        sent.append(copy)
        flying[key] = copy

    def landed(key, copy):
        copy.wait_recv()
        del flying[key]

    part_swaps = []

    def partial_keys(k):
        off, rows = CHUNKS[k]
        loads[1 + k].wait()
        at = pl.ds(off, rows)
        for side, place in ((1 - core, part_out), (core, part_own)):
            x_rows = xv[:, side, at, :].reshape(NZ * rows, WIDTH)
            part = dot(x_rows, wv[...], ((1,), (1,)))
            place[:, at, :] = part.astype(BF).reshape(NZ, rows, KV)

    def swap_parts(k):
        at = (slice(None), pl.ds(*CHUNKS[k]))
        part_swaps.append(remote(part_out.at[at], part_in.at[at], ps_s.at[k], ps_r.at[k], sib))
        start(("ps", k), part_swaps[k])

    loads[0].wait()
    partial_keys(0)
    pl.semaphore_wait(barrier, len(near) + len(far))
    for way, (step, half) in enumerate(WAYS):
        start(("cr", way), remote(
            cot_hbm.at[FEATURES[way], window((zh + 2) % NZ)], cot_relay.at[way], cr_s.at[way], cr_r.at[way], z_peer(step)
        ))
    for way, (step, half) in enumerate(WAYS):
        start(("cz", way), remote(
            cot_hbm.at[:, window((zh + step) % NZ)], cot_in.at[zh, core], cz_s.at[way], cz_r.at[way], z_peer(step)
        ))
    swap_parts(0)
    for k in range(1, len(CHUNKS)):
        partial_keys(k)
        swap_parts(k)
    heralds = [y_peer(2), y_peer(6), x_peer(2, 0)]
    for peer in heralds:
        pl.semaphore_signal(heard, inc=1, device_id=peer, device_id_type=MESH)

    for k, (off, rows) in enumerate(CHUNKS):
        at = pl.ds(off, rows)
        landed(("ps", k), part_swaps[k])
        pair[:, at, :] = (part_own[:, at, :].astype(F32) + part_in[:, at, :].astype(F32)).astype(BF)
        for way, (step, half) in enumerate(WAYS):
            start(("r1", k, way), remote(
                pair.at[(zh + 2) % NZ, at, half], relay.at[way, at], r1_s.at[k, way], r1_r.at[k, way], z_peer(step)
            ))

    for k, (off, rows) in enumerate(CHUNKS):
        at = pl.ds(off, rows)
        for way, (step, half) in enumerate(WAYS):
            other = WAYS[1 - way][1]
            start(("rd", k, way), remote(
                pair.at[(zh + step) % NZ, at, other], recv.at[way, at, other],
                rd_s.at[k, way], rd_r.at[k, way], z_peer(step),
            ))
    for load in loads[base + 1 :]:
        load.wait()
    mom_new[...] = DECAY * momv[0].astype(F32)
    leftv[...] = left_f[...].astype(BF)
    left_tv[...] = left_t_f[...].astype(BF)
    for way, (step, half) in enumerate(WAYS):
        landed(("cr", way), remote(cot_relay.at[way], cot_relay.at[way], cr_s.at[way], cr_r.at[way], sib))
        start(("cf", way), remote(
            cot_relay.at[way], cot_in.at[(zh + NZ - step) % NZ, core, FEATURES[way]], cf_s.at[way], cf_r.at[way], z_peer(step)
        ))
    for k, (off, rows) in enumerate(CHUNKS):
        at = pl.ds(off, rows)
        for way, (step, half) in enumerate(WAYS):
            landed(("r1", k, way), remote(
                pair.at[0, at, half], relay.at[way, at], r1_s.at[k, way], r1_r.at[k, way], sib
            ))
            both = pair[(zh + step) % NZ, at, half].astype(F32) + relay[way, at, :].astype(F32)
            relay_sum[way, at, :] = both.astype(BF)
            start(("r2", k, way), remote(
                relay_sum.at[way, at], recv.at[way, at, half], r2_s.at[k, way], r2_r.at[k, way], z_peer(step)
            ))

    block_r = lax.broadcasted_iota(jnp.int32, (BAND, WIDTH), 1) // SPAN
    block_c = lax.broadcasted_iota(jnp.int32, (BAND, LANES), 1) // BAND

    def spread(r, carry):
        of_row = jnp.zeros((BAND, WIDTH), jnp.int32)
        of_col = jnp.zeros((BAND, LANES), jnp.int32)
        for c in range(COLS_BLK):
            of_row = jnp.where(block_r == c, row_ref[r, c], of_row)
            of_col = jnp.where(block_c == c, col_ref[r, c], of_col)
        row_mask[r] = of_row
        col_mask[r] = of_col
        return carry

    lax.fori_loop(0, ROWS_BLK, spread, 0)
    loads[base].wait()
    for way, (step, half) in enumerate(WAYS):
        got = cot_in.at[(zh + NZ - step) % NZ, core]
        landed(("cz", way), remote(got, got, cz_s.at[way], cz_r.at[way], sib))
        got = cot_in.at[(zh + 2) % NZ, core, FEATURES[way]]
        landed(("cf", way), remote(got, got, cf_s.at[way], cf_r.at[way], sib))
    start(("cs",), remote(cot_in.at[:, core], cot_in.at[:, core], cs_s, cs_r, sib))
    landed(("cs",), remote(cot_in.at[:, 1 - core], cot_in.at[:, 1 - core], cs_s, cs_r, sib))
    cot_t[...] = cot_in[...].reshape(KV, WINDOW).T.astype(F32)
    cot_base = pl.multiple_of((zh % 2) * 64 + core * OWN, 32)
    gain = gain_ref[...]
    for k, (off, rows) in enumerate(CHUNKS):
        at = pl.ds(off, rows)
        for way, (step, half) in enumerate(WAYS):
            other = WAYS[1 - way][1]
            landed(("rd", k, way), remote(
                pair.at[0, at, other], recv.at[way, at, other], rd_s.at[k, way], rd_r.at[k, way], sib
            ))
        for way, (step, half) in enumerate(WAYS):
            landed(("r2", k, way), remote(
                relay_sum.at[way, at], recv.at[way, at, half], r2_s.at[k, way], r2_r.at[k, way], sib
            ))
        keys = pair[zh, at, :].astype(F32) + recv[0, at, :].astype(F32) + recv[1, at, :].astype(F32)
        scaled = gain * cot_t[pl.ds(cot_base + off, rows), :]
        inverse = lax.rsqrt(jnp.mean(keys * keys, axis=-1, keepdims=True) + EPS)
        inner = jnp.sum(scaled * keys, axis=-1, keepdims=True)
        dk[mp, at, :] = (inverse * scaled - (inverse * inverse * inverse * inner / KV) * keys).astype(BF)
        mine = dk.at[mp, at]
        for way, (step, half) in enumerate(WAYS):
            start(("ag", k, way), remote(mine, mine, ag_s.at[k, way], ag_r.at[k, way], z_peer(step)))
        start(("fw", k, 0), remote(mine, mine, fw_s.at[k, 0], fw_r.at[k, 0], sib))

    lane_block = (lax.broadcasted_iota(jnp.int32, (SPAN, OFFSETS * LANES), 1) % LANES) // BAND
    for c in range(COLS_BLK):
        for part in range(2):
            rightv[part, c * SPAN : (c + 1) * SPAN] = jnp.where(lane_block == c, right_f[part], 0.0).astype(BF)

    def owner(step, side):
        return ((zh + NZ - step) % NZ) * 2 + side

    for k, (off, rows) in enumerate(CHUNKS):
        at = pl.ds(off, rows)
        for way, (step, half) in enumerate(WAYS):
            got = dk.at[owner(step, core), at]
            landed(("ag", k, way), remote(got, got, ag_s.at[k, way], ag_r.at[k, way], sib))
            part = dk.at[owner(step, core), at, half]
            start(("a2", k, way), remote(part, part, a2_s.at[k, way], a2_r.at[k, way], z_peer(step)))
            start(("fw", k, step), remote(got, got, fw_s.at[k, step], fw_r.at[k, step], sib))
    def wait_other_core(k, step):
        got = dk.at[owner(step, 1 - core), pl.ds(*CHUNKS[k])]
        landed(("fw", k, step), remote(got, got, fw_s.at[k, step], fw_r.at[k, step], sib))

    def part_gradient(k, steps):
        off, rows = CHUNKS[k]
        chips = [(zh + NZ - step) % NZ for step in steps]
        some_dk = [dk[pl.ds(2 * chip, 2), pl.ds(off, rows), :].reshape(2 * rows, KV) for chip in chips]
        some_x = [xv[chip, :, pl.ds(off, rows), :].reshape(2 * rows, WIDTH) for chip in chips]
        some_dk, some_x = jnp.concatenate(some_dk, axis=0), jnp.concatenate(some_x, axis=0)
        return dot(some_dk, some_x, ((0,), (0,))) * (1.0 / math.sqrt(2 * NZ * OWN))

    last = len(CHUNKS) - 1
    for k in range(len(CHUNKS)):
        for step in (0, 1, 3):
            wait_other_core(k, step)
        mom_new[...] += part_gradient(k, (0, 1, 3))
    for k, (off, rows) in enumerate(CHUNKS):
        at = pl.ds(off, rows)
        for way, (step, half) in enumerate(WAYS):
            part = dk.at[owner(2, core), at, half]
            landed(("a2", k, way), remote(part, part, a2_s.at[k, way], a2_r.at[k, way], sib))
        got = dk.at[owner(2, core), at]
        start(("fw", k, 2), remote(got, got, fw_s.at[k, 2], fw_r.at[k, 2], sib))
        if k == last:
            for g in range(2):
                high, low = split(mom_new[g * 256 : (g + 1) * 256, :])
                both = dot(leftv[...], high)
                sections[g] = both[:128] + both[128:] + dot(leftv[:128], low)
        wait_other_core(k, 2)
        if k < last:
            mom_new[...] += part_gradient(k, (2,))
    last_piece = part_gradient(last, (2,))

    picked = []
    for g in range(2):
        both = dot(leftv[...], last_piece[g * 256 : (g + 1) * 256].astype(BF))
        sect = (sections[g] + both[:128] + both[128:]).reshape(4, OFFSETS, BAND, WIDTH)
        chosen = row_mask[g * 4 : (g + 1) * 4]
        total = jnp.zeros((4, BAND, WIDTH), F32)
        for band in range(OFFSETS):
            total = total + jnp.where(chosen == band, sect[:, band], 0.0)
        picked.append(total.reshape(32, WIDTH))
    sect = jnp.concatenate(picked, axis=0)
    high, low = split(sect)
    both = dot(jnp.concatenate([high, low], axis=0), rightv[0])
    full = both[:64] + both[64:] + dot(high, rightv[1])
    chosen = col_mask[...].reshape(64, LANES)
    coeffs = jnp.zeros((64, LANES), F32)
    for band in range(OFFSETS):
        coeffs = coeffs + jnp.where(chosen == band, full[:, band * LANES : (band + 1) * LANES], 0.0)

    band_y[y] = coeffs.astype(BF)
    pl.semaphore_wait(heard, len(heralds))
    for step in (4, 3, 5, 2, 6, 1, 7):
        start(("y", step), remote(band_y.at[y], band_y.at[y], y_s.at[step - 1], y_r.at[step - 1], y_peer(step)))

    mom_new[...] += last_piece
    def rebuild(values, exact, put):
        parts = [jnp.where(chosen == band, values, 0.0) for band in range(OFFSETS)]
        high, low = split(jnp.concatenate(parts, axis=1))
        if exact:
            both = dot(jnp.concatenate([high, low], axis=0), rightv[0], ((1,), (1,)))
            first = both[:64] + both[64:] + dot(high, rightv[1], ((1,), (1,)))
        else:
            first = dot(high, rightv[0], ((1,), (1,)))
        for g in range(2):
            rows = first[g * 32 : (g + 1) * 32].reshape(4, 1, BAND, WIDTH)
            bands = lax.broadcasted_iota(jnp.int32, (4, OFFSETS, BAND, WIDTH), 1)
            mask = row_mask[g * 4 : (g + 1) * 4].reshape(4, 1, BAND, WIDTH)
            spread_rows = jnp.where(mask == bands, rows, 0.0).reshape(128, WIDTH)
            high, low = split(spread_rows)
            out = dot(left_tv[0], high)
            if exact:
                out = out + dot(left_tv[1], high) + dot(left_tv[0], low)
            put(g, out)

    def put_new(g, own):
        at = slice(g * 256, (g + 1) * 256)
        new_v[0, at, :] = (mom_new[at, :] - own).astype(BF)

    rebuild(coeffs, True, put_new)

    for step in (1, 7, 2, 6, 3, 5, 4):
        got = band_y.at[(y + NY - step) % NY]
        landed(("y", step), remote(got, got, y_s.at[step - 1], y_r.at[step - 1], sib))
    total = band_y[0].astype(F32)
    for j in range(1, NY):
        total = total + band_y[j].astype(F32)
    band_xz[xz] = total.astype(BF)
    for step in range(1, NXZ):
        start(("xz", step), remote(band_xz.at[xz], band_xz.at[xz], xz_s.at[step - 1], xz_r.at[step - 1], xz_peer(step)))
    for step in range(1, NXZ):
        got = band_xz.at[(xz + NXZ - step) % NXZ]
        landed(("xz", step), remote(got, got, xz_s.at[step - 1], xz_r.at[step - 1], sib))
    total = band_xz[0].astype(F32)
    for j in range(1, NXZ):
        total = total + band_xz[j].astype(F32)

    def put_update(g, value):
        upd_v[g * 256 : (g + 1) * 256, :] = value.astype(BF)

    rebuild(total * (1.0 / N_DP), False, put_update)
    for copy in sent:
        copy.wait_send()


def hbm(value):
    return pltpu.with_memory_space_constraint(value, pltpu.HBM)


def on_device(tokens, key_weight, key_gain, cotangent, momentum, band_row, band_col):
    left, left_t, right = tables()
    n = len(CHUNKS)
    any_spec = pl.BlockSpec(memory_space=pltpu.HBM)
    vmem = pl.BlockSpec(memory_space=pltpu.VMEM)
    dma = pltpu.SemaphoreType.DMA
    return pl.pallas_call(
        kernel,
        out_shape=(
            jax.ShapeDtypeStruct((KV, WIDTH), BF),
            jax.ShapeDtypeStruct((1, KV, WIDTH), BF),
        ),
        in_specs=[any_spec] * 10,
        out_specs=(vmem, vmem),
        scratch_shapes=[
            pltpu.VMEM((NZ, 2, OWN, WIDTH), BF),
            pltpu.VMEM((KV, WIDTH), BF),
            pltpu.VMEM((1, KV), F32),
            pltpu.SMEM((ROWS_BLK, COLS_BLK), jnp.int32),
            pltpu.SMEM((ROWS_BLK, COLS_BLK), jnp.int32),
            pltpu.VMEM((1, KV, WIDTH), BF),
            pltpu.VMEM(left.shape, F32),
            pltpu.VMEM(left_t.shape, F32),
            pltpu.VMEM(right.shape, F32),
            pltpu.VMEM(left.shape, BF),
            pltpu.VMEM(left_t.shape, BF),
            pltpu.VMEM((2, WIDTH, OFFSETS * LANES), BF),
            pltpu.VMEM((NZ, 2, KV // (2 * NZ), WINDOW), BF),
            pltpu.VMEM((2, KV // (4 * NZ), WINDOW), BF),
            pltpu.VMEM((WINDOW, KV), F32),
            pltpu.VMEM((NZ, OWN, KV), BF),
            pltpu.VMEM((NZ, OWN, KV), BF),
            pltpu.VMEM((NZ, OWN, KV), BF),
            pltpu.VMEM((NZ, OWN, KV), BF),
            pltpu.VMEM((2, OWN, KV // 2), BF),
            pltpu.VMEM((2, OWN, KV // 2), BF),
            pltpu.VMEM((2, OWN, KV), BF),
            pltpu.VMEM((2 * NZ, OWN, KV), BF),
            pltpu.VMEM((KV, WIDTH), F32),
            pltpu.VMEM((2, 128, WIDTH), F32),
            pltpu.VMEM((ROWS_BLK, BAND, WIDTH), jnp.int32),
            pltpu.VMEM((ROWS_BLK, BAND, LANES), jnp.int32),
            pltpu.VMEM((NY, 64, LANES), BF),
            pltpu.VMEM((NXZ, 64, LANES), BF),
            dma((9 + n,)),
            dma(()),
            dma(()),
            dma((2,)),
            dma((2,)),
            dma((2,)),
            dma((2,)),
            dma((2,)),
            dma((2,)),
            dma((n,)),
            dma((n,)),
            dma((n, 2)),
            dma((n, 2)),
            dma((n, 2)),
            dma((n, 2)),
            dma((n, 2)),
            dma((n, 2)),
            dma((n, 2)),
            dma((n, 2)),
            dma((n, 2)),
            dma((n, 2)),
            dma((n, 4)),
            dma((n, 4)),
            dma((7,)),
            dma((7,)),
            dma((7,)),
            dma((7,)),
            pltpu.SemaphoreType.REGULAR,
        ],
        compiler_params=pltpu.CompilerParams(
            collective_id=0, has_side_effects=True, vmem_limit_bytes=48 * 1024 * 1024
        ),
        cost_estimate=pl.CostEstimate(flops=2_500_000_000, bytes_accessed=6_000_000, transcendentals=1280),
    )(
        hbm(tokens.reshape(NZ, 2, OWN, WIDTH)),
        hbm(key_weight),
        hbm(key_gain.reshape(1, KV)),
        hbm(cotangent.T),
        hbm(momentum),
        hbm(band_row),
        hbm(band_col),
        hbm(left),
        hbm(left_t),
        hbm(right),
    )


def solution(mesh):
    return jax.shard_map(
        on_device,
        mesh=mesh,
        in_specs=(
            P("dp", "mp"),
            P(None, "mp"),
            P(),
            P("dp", "mp"),
            P("dp", None, "mp"),
            P(None, "mp"),
            P(None, "mp"),
        ),
        out_specs=(P(None, "mp"), P("dp", None, "mp")),
        check_vma=False,
    )
```

```python
import math

import jax
import jax.numpy as jnp
import ml_dtypes
import numpy as np
from jax import lax
from jax.experimental import pallas as pl
from jax.experimental.pallas import tpu as pltpu
from jax.sharding import PartitionSpec as P

MESH = pl.DeviceIdType.MESH
BF = jnp.bfloat16
F32 = jnp.float32

SPAN = 64
BAND = 8
OFFSETS = 4
LOW = BAND * OFFSETS
EPS = 1e-06
DECAY = 0.9

NY = 8
NXZ = 8
NZ = 4
N_DP = NY * NXZ
OWN = 160
KV = 512
WIDTH = 640
ROWS_BLK = KV // SPAN
COLS_BLK = WIDTH // SPAN
LANES = 128
WINDOW = 3 * LANES
CHUNKS = ((0, 48), (48, 112))
FEATURES = (slice(0, 32), slice(32, 64))
WAYS = ((1, slice(0, 256)), (3, slice(256, 512)))


def split_const(table):
    high = table.astype(np.float32).astype(ml_dtypes.bfloat16)
    low = (table - high.astype(np.float64)).astype(np.float32).astype(ml_dtypes.bfloat16)
    return high.astype(np.float32), low.astype(np.float32)


def tables():
    f = np.arange(SPAN, dtype=np.float64)[:, None]
    n = np.arange(SPAN, dtype=np.float64)[None, :]
    c = np.cos(np.pi * (2.0 * n + 1.0) * f / (2.0 * SPAN))
    c = c * np.where(f == 0, np.sqrt(1.0 / SPAN), np.sqrt(2.0 / SPAN))
    c = c[:LOW]
    high, low = split_const(np.kron(np.eye(4), c))
    right = np.zeros((SPAN, OFFSETS, LANES // BAND, BAND))
    right[:] = c.T.reshape(SPAN, OFFSETS, 1, BAND)
    return (
        np.concatenate([high, low], axis=0),
        np.stack([np.ascontiguousarray(high.T), np.ascontiguousarray(low.T)]),
        np.stack(split_const(right.reshape(SPAN, OFFSETS * LANES))),
    )


def dot(a, b, dims=((1,), (0,))):
    return lax.dot_general(a, b, (dims, ((), ())), preferred_element_type=F32)


def split(value):
    high = value.astype(BF)
    return high, (value - high.astype(F32)).astype(BF)


def kernel(
    x_hbm, w_hbm, gain_hbm, cot_hbm, mom_hbm, row_hbm, col_hbm, left_hbm, left_t_hbm, right_hbm,
    upd_v, new_v,
    xv, wv, gain_ref, row_ref, col_ref, momv, left_f, left_t_f, right_f, leftv, left_tv, rightv,
    cot_in, cot_relay, cot_t, part_out, part_own, part_in, pair, relay, relay_sum, recv, dk, mom_new, sections,
    row_mask, col_mask, band_y, band_xz,
    load_sem, cs_s, cs_r, cr_s, cr_r, cf_s, cf_r, cz_s, cz_r, ps_s, ps_r, r1_s, r1_r, rd_s, rd_r, r2_s, r2_r, ag_s, ag_r, a2_s, a2_r, fw_s, fw_r,
    y_s, y_r, xz_s, xz_r, heard,
):
    dp = lax.axis_index("dp")
    mp = lax.axis_index("mp")
    zh = mp // 2
    core = mp % 2
    y = dp % NY
    xz = dp // NY
    sib = {"dp": dp, "mp": zh * 2 + (1 - core)}

    def z_peer(step):
        return {"dp": dp, "mp": ((zh + step) % NZ) * 2 + core}

    def y_peer(step):
        return {"dp": xz * NY + (y + step) % NY, "mp": mp}

    def xz_peer(step):
        return {"dp": ((xz + step) % NXZ) * NY + y, "mp": mp}

    barrier = pltpu.get_barrier_semaphore()
    def x_peer(step, flip):
        return {"dp": (((xz // 2 + step) % (NXZ // 2)) * 2 + (xz % 2 + flip) % 2) * NY + y, "mp": mp}

    near = [z_peer(1), z_peer(3), sib]
    far = [y_peer(s) for s in (2, 6, 1, 7)]
    far += [x_peer(2, 0), x_peer(1, 1), x_peer(3, 1), x_peer(1, 0), x_peer(3, 0), x_peer(0, 1)]

    def greet(peers):
        for peer in peers:
            pl.semaphore_signal(barrier, inc=1, device_id=peer, device_id_type=MESH)

    greet(near)
    loads = [pltpu.make_async_copy(w_hbm, wv, load_sem.at[0])]
    for k, (off, rows) in enumerate(CHUNKS):
        at = (slice(None), slice(None), pl.ds(off, rows))
        loads.append(pltpu.make_async_copy(x_hbm.at[at], xv.at[at], load_sem.at[1 + k]))
    base = 1 + len(CHUNKS)
    more = [(cot_hbm.at[:, pl.ds(pl.multiple_of((zh * 5 // 2) * LANES, LANES), WINDOW)], cot_in.at[zh, core]), (gain_hbm, gain_ref), (row_hbm, row_ref), (col_hbm, col_ref), (mom_hbm, momv)]
    more += [(left_hbm, left_f), (left_t_hbm, left_t_f), (right_hbm, right_f)]
    for k, (src, dst) in enumerate(more):
        loads.append(pltpu.make_async_copy(src, dst, load_sem.at[base + k]))
    for load in loads[: base + 1]:
        load.start()
    greet(far)
    for load in loads[base + 1 :]:
        load.start()

    def window(chip):
        return pl.ds(pl.multiple_of((chip * 5 // 2) * LANES, LANES), WINDOW)

    def remote(src, dst, send, recv_, peer):
        return pltpu.make_async_remote_copy(
            src_ref=src, dst_ref=dst, send_sem=send, recv_sem=recv_, device_id=peer, device_id_type=MESH
        )

    sent = []
    flying = {}

    def start(key, copy):
        copy.start()
        sent.append(copy)
        flying[key] = copy

    def landed(key, copy):
        copy.wait_recv()
        del flying[key]

    part_swaps = []

    def partial_keys(k):
        off, rows = CHUNKS[k]
        loads[1 + k].wait()
        at = pl.ds(off, rows)
        for side, place in ((1 - core, part_out), (core, part_own)):
            x_rows = xv[:, side, at, :].reshape(NZ * rows, WIDTH)
            part = dot(x_rows, wv[...], ((1,), (1,)))
            place[:, at, :] = part.astype(BF).reshape(NZ, rows, KV)

    def swap_parts(k):
        at = (slice(None), pl.ds(*CHUNKS[k]))
        part_swaps.append(remote(part_out.at[at], part_in.at[at], ps_s.at[k], ps_r.at[k], sib))
        start(("ps", k), part_swaps[k])

    loads[0].wait()
    partial_keys(0)
    pl.semaphore_wait(barrier, len(near) + len(far))
    for way, (step, half) in enumerate(WAYS):
        start(("cr", way), remote(
            cot_hbm.at[FEATURES[way], window((zh + 2) % NZ)], cot_relay.at[way], cr_s.at[way], cr_r.at[way], z_peer(step)
        ))
    for way, (step, half) in enumerate(WAYS):
        start(("cz", way), remote(
            cot_hbm.at[:, window((zh + step) % NZ)], cot_in.at[zh, core], cz_s.at[way], cz_r.at[way], z_peer(step)
        ))
    swap_parts(0)
    for k in range(1, len(CHUNKS)):
        partial_keys(k)
        swap_parts(k)
    heralds = [y_peer(2), y_peer(6), x_peer(2, 0)]
    for peer in heralds:
        pl.semaphore_signal(heard, inc=1, device_id=peer, device_id_type=MESH)

    for k, (off, rows) in enumerate(CHUNKS):
        at = pl.ds(off, rows)
        landed(("ps", k), part_swaps[k])
        pair[:, at, :] = (part_own[:, at, :].astype(F32) + part_in[:, at, :].astype(F32)).astype(BF)
        for way, (step, half) in enumerate(WAYS):
            start(("r1", k, way), remote(
                pair.at[(zh + 2) % NZ, at, half], relay.at[way, at], r1_s.at[k, way], r1_r.at[k, way], z_peer(step)
            ))

    for k, (off, rows) in enumerate(CHUNKS):
        at = pl.ds(off, rows)
        for way, (step, half) in enumerate(WAYS):
            other = WAYS[1 - way][1]
            start(("rd", k, way), remote(
                pair.at[(zh + step) % NZ, at, other], recv.at[way, at, other],
                rd_s.at[k, way], rd_r.at[k, way], z_peer(step),
            ))
    for load in loads[base + 1 :]:
        load.wait()
    mom_new[...] = DECAY * momv[0].astype(F32)
    leftv[...] = left_f[...].astype(BF)
    left_tv[...] = left_t_f[...].astype(BF)
    for way, (step, half) in enumerate(WAYS):
        landed(("cr", way), remote(cot_relay.at[way], cot_relay.at[way], cr_s.at[way], cr_r.at[way], sib))
        start(("cf", way), remote(
            cot_relay.at[way], cot_in.at[(zh + NZ - step) % NZ, core, FEATURES[way]], cf_s.at[way], cf_r.at[way], z_peer(step)
        ))
    for k, (off, rows) in enumerate(CHUNKS):
        at = pl.ds(off, rows)
        for way, (step, half) in enumerate(WAYS):
            landed(("r1", k, way), remote(
                pair.at[0, at, half], relay.at[way, at], r1_s.at[k, way], r1_r.at[k, way], sib
            ))
            both = pair[(zh + step) % NZ, at, half].astype(F32) + relay[way, at, :].astype(F32)
            relay_sum[way, at, :] = both.astype(BF)
            start(("r2", k, way), remote(
                relay_sum.at[way, at], recv.at[way, at, half], r2_s.at[k, way], r2_r.at[k, way], z_peer(step)
            ))

    block_r = lax.broadcasted_iota(jnp.int32, (BAND, WIDTH), 1) // SPAN
    block_c = lax.broadcasted_iota(jnp.int32, (BAND, LANES), 1) // BAND

    def spread(r, carry):
        of_row = jnp.zeros((BAND, WIDTH), jnp.int32)
        of_col = jnp.zeros((BAND, LANES), jnp.int32)
        for c in range(COLS_BLK):
            of_row = jnp.where(block_r == c, row_ref[r, c], of_row)
            of_col = jnp.where(block_c == c, col_ref[r, c], of_col)
        row_mask[r] = of_row
        col_mask[r] = of_col
        return carry

    lax.fori_loop(0, ROWS_BLK, spread, 0)
    loads[base].wait()
    for way, (step, half) in enumerate(WAYS):
        got = cot_in.at[(zh + NZ - step) % NZ, core]
        landed(("cz", way), remote(got, got, cz_s.at[way], cz_r.at[way], sib))
        got = cot_in.at[(zh + 2) % NZ, core, FEATURES[way]]
        landed(("cf", way), remote(got, got, cf_s.at[way], cf_r.at[way], sib))
    start(("cs",), remote(cot_in.at[:, core], cot_in.at[:, core], cs_s, cs_r, sib))
    landed(("cs",), remote(cot_in.at[:, 1 - core], cot_in.at[:, 1 - core], cs_s, cs_r, sib))
    cot_t[...] = cot_in[...].reshape(KV, WINDOW).T.astype(F32)
    cot_base = pl.multiple_of((zh % 2) * 64 + core * OWN, 32)
    gain = gain_ref[...]
    for k, (off, rows) in enumerate(CHUNKS):
        at = pl.ds(off, rows)
        for way, (step, half) in enumerate(WAYS):
            other = WAYS[1 - way][1]
            landed(("rd", k, way), remote(
                pair.at[0, at, other], recv.at[way, at, other], rd_s.at[k, way], rd_r.at[k, way], sib
            ))
        for way, (step, half) in enumerate(WAYS):
            landed(("r2", k, way), remote(
                relay_sum.at[way, at], recv.at[way, at, half], r2_s.at[k, way], r2_r.at[k, way], sib
            ))
        keys = pair[zh, at, :].astype(F32) + recv[0, at, :].astype(F32) + recv[1, at, :].astype(F32)
        scaled = gain * cot_t[pl.ds(cot_base + off, rows), :]
        inverse = lax.rsqrt(jnp.mean(keys * keys, axis=-1, keepdims=True) + EPS)
        inner = jnp.sum(scaled * keys, axis=-1, keepdims=True)
        dk[mp, at, :] = (inverse * scaled - (inverse * inverse * inverse * inner / KV) * keys).astype(BF)
        mine = dk.at[mp, at]
        for way, (step, half) in enumerate(WAYS):
            start(("ag", k, way), remote(mine, mine, ag_s.at[k, way], ag_r.at[k, way], z_peer(step)))
        start(("fw", k, 0), remote(mine, mine, fw_s.at[k, 0], fw_r.at[k, 0], sib))

    lane_block = (lax.broadcasted_iota(jnp.int32, (SPAN, OFFSETS * LANES), 1) % LANES) // BAND
    for c in range(COLS_BLK):
        for part in range(2):
            rightv[part, c * SPAN : (c + 1) * SPAN] = jnp.where(lane_block == c, right_f[part], 0.0).astype(BF)

    def owner(step, side):
        return ((zh + NZ - step) % NZ) * 2 + side

    for k, (off, rows) in enumerate(CHUNKS):
        at = pl.ds(off, rows)
        for way, (step, half) in enumerate(WAYS):
            got = dk.at[owner(step, core), at]
            landed(("ag", k, way), remote(got, got, ag_s.at[k, way], ag_r.at[k, way], sib))
            part = dk.at[owner(step, core), at, half]
            start(("a2", k, way), remote(part, part, a2_s.at[k, way], a2_r.at[k, way], z_peer(step)))
            start(("fw", k, step), remote(got, got, fw_s.at[k, step], fw_r.at[k, step], sib))
    def wait_other_core(k, step):
        got = dk.at[owner(step, 1 - core), pl.ds(*CHUNKS[k])]
        landed(("fw", k, step), remote(got, got, fw_s.at[k, step], fw_r.at[k, step], sib))

    def part_gradient(k, steps):
        off, rows = CHUNKS[k]
        chips = [(zh + NZ - step) % NZ for step in steps]
        some_dk = [dk[pl.ds(2 * chip, 2), pl.ds(off, rows), :].reshape(2 * rows, KV) for chip in chips]
        some_x = [xv[chip, :, pl.ds(off, rows), :].reshape(2 * rows, WIDTH) for chip in chips]
        some_dk, some_x = jnp.concatenate(some_dk, axis=0), jnp.concatenate(some_x, axis=0)
        return dot(some_dk, some_x, ((0,), (0,))) * (1.0 / math.sqrt(2 * NZ * OWN))

    last = len(CHUNKS) - 1
    for k in range(len(CHUNKS)):
        for step in (0, 1, 3):
            wait_other_core(k, step)
        mom_new[...] += part_gradient(k, (0, 1, 3))
    for k, (off, rows) in enumerate(CHUNKS):
        at = pl.ds(off, rows)
        for way, (step, half) in enumerate(WAYS):
            part = dk.at[owner(2, core), at, half]
            landed(("a2", k, way), remote(part, part, a2_s.at[k, way], a2_r.at[k, way], sib))
        got = dk.at[owner(2, core), at]
        start(("fw", k, 2), remote(got, got, fw_s.at[k, 2], fw_r.at[k, 2], sib))
        if k == last:
            for g in range(2):
                high, low = split(mom_new[g * 256 : (g + 1) * 256, :])
                both = dot(leftv[...], high)
                sections[g] = both[:128] + both[128:] + dot(leftv[:128], low)
        wait_other_core(k, 2)
        if k < last:
            mom_new[...] += part_gradient(k, (2,))
    last_piece = part_gradient(last, (2,))

    picked = []
    for g in range(2):
        both = dot(leftv[...], last_piece[g * 256 : (g + 1) * 256].astype(BF))
        sect = (sections[g] + both[:128] + both[128:]).reshape(4, OFFSETS, BAND, WIDTH)
        chosen = row_mask[g * 4 : (g + 1) * 4]
        total = jnp.zeros((4, BAND, WIDTH), F32)
        for band in range(OFFSETS):
            total = total + jnp.where(chosen == band, sect[:, band], 0.0)
        picked.append(total.reshape(32, WIDTH))
    sect = jnp.concatenate(picked, axis=0)
    high, low = split(sect)
    both = dot(jnp.concatenate([high, low], axis=0), rightv[0])
    full = both[:64] + both[64:] + dot(high, rightv[1])
    chosen = col_mask[...].reshape(64, LANES)
    coeffs = jnp.zeros((64, LANES), F32)
    for band in range(OFFSETS):
        coeffs = coeffs + jnp.where(chosen == band, full[:, band * LANES : (band + 1) * LANES], 0.0)

    band_y[y] = coeffs.astype(BF)
    pl.semaphore_wait(heard, len(heralds))
    for step in (4, 3, 5, 2, 6, 1, 7):
        start(("y", step), remote(band_y.at[y], band_y.at[y], y_s.at[step - 1], y_r.at[step - 1], y_peer(step)))

    mom_new[...] += last_piece
    def rebuild(values, exact, put):
        parts = [jnp.where(chosen == band, values, 0.0) for band in range(OFFSETS)]
        high, low = split(jnp.concatenate(parts, axis=1))
        if exact:
            both = dot(jnp.concatenate([high, low], axis=0), rightv[0], ((1,), (1,)))
            first = both[:64] + both[64:] + dot(high, rightv[1], ((1,), (1,)))
        else:
            first = dot(high, rightv[0], ((1,), (1,)))
        for g in range(2):
            rows = first[g * 32 : (g + 1) * 32].reshape(4, 1, BAND, WIDTH)
            bands = lax.broadcasted_iota(jnp.int32, (4, OFFSETS, BAND, WIDTH), 1)
            mask = row_mask[g * 4 : (g + 1) * 4].reshape(4, 1, BAND, WIDTH)
            spread_rows = jnp.where(mask == bands, rows, 0.0).reshape(128, WIDTH)
            high, low = split(spread_rows)
            out = dot(left_tv[0], high)
            if exact:
                out = out + dot(left_tv[1], high) + dot(left_tv[0], low)
            put(g, out)

    def put_new(g, own):
        at = slice(g * 256, (g + 1) * 256)
        new_v[0, at, :] = (mom_new[at, :] - own).astype(BF)

    rebuild(coeffs, True, put_new)

    for step in (1, 7, 2, 6, 3, 5, 4):
        got = band_y.at[(y + NY - step) % NY]
        landed(("y", step), remote(got, got, y_s.at[step - 1], y_r.at[step - 1], sib))
    total = band_y[0].astype(F32)
    for j in range(1, NY):
        total = total + band_y[j].astype(F32)
    band_xz[xz] = total.astype(BF)
    for step in range(1, NXZ):
        start(("xz", step), remote(band_xz.at[xz], band_xz.at[xz], xz_s.at[step - 1], xz_r.at[step - 1], xz_peer(step)))
    for step in range(1, NXZ):
        got = band_xz.at[(xz + NXZ - step) % NXZ]
        landed(("xz", step), remote(got, got, xz_s.at[step - 1], xz_r.at[step - 1], sib))
    total = band_xz[0].astype(F32)
    for j in range(1, NXZ):
        total = total + band_xz[j].astype(F32)

    def put_update(g, value):
        upd_v[g * 256 : (g + 1) * 256, :] = value.astype(BF)

    rebuild(total * (1.0 / N_DP), False, put_update)
    for copy in sent:
        copy.wait_send()


def hbm(value):
    return pltpu.with_memory_space_constraint(value, pltpu.HBM)


def on_device(tokens, key_weight, key_gain, cotangent, momentum, band_row, band_col):
    left, left_t, right = tables()
    n = len(CHUNKS)
    any_spec = pl.BlockSpec(memory_space=pltpu.HBM)
    vmem = pl.BlockSpec(memory_space=pltpu.VMEM)
    dma = pltpu.SemaphoreType.DMA
    return pl.pallas_call(
        kernel,
        out_shape=(
            jax.ShapeDtypeStruct((KV, WIDTH), BF),
            jax.ShapeDtypeStruct((1, KV, WIDTH), BF),
        ),
        in_specs=[any_spec] * 10,
        out_specs=(vmem, vmem),
        scratch_shapes=[
            pltpu.VMEM((NZ, 2, OWN, WIDTH), BF),
            pltpu.VMEM((KV, WIDTH), BF),
            pltpu.VMEM((1, KV), F32),
            pltpu.SMEM((ROWS_BLK, COLS_BLK), jnp.int32),
            pltpu.SMEM((ROWS_BLK, COLS_BLK), jnp.int32),
            pltpu.VMEM((1, KV, WIDTH), BF),
            pltpu.VMEM(left.shape, F32),
            pltpu.VMEM(left_t.shape, F32),
            pltpu.VMEM(right.shape, F32),
            pltpu.VMEM(left.shape, BF),
            pltpu.VMEM(left_t.shape, BF),
            pltpu.VMEM((2, WIDTH, OFFSETS * LANES), BF),
            pltpu.VMEM((NZ, 2, KV // (2 * NZ), WINDOW), BF),
            pltpu.VMEM((2, KV // (4 * NZ), WINDOW), BF),
            pltpu.VMEM((WINDOW, KV), F32),
            pltpu.VMEM((NZ, OWN, KV), BF),
            pltpu.VMEM((NZ, OWN, KV), BF),
            pltpu.VMEM((NZ, OWN, KV), BF),
            pltpu.VMEM((NZ, OWN, KV), BF),
            pltpu.VMEM((2, OWN, KV // 2), BF),
            pltpu.VMEM((2, OWN, KV // 2), BF),
            pltpu.VMEM((2, OWN, KV), BF),
            pltpu.VMEM((2 * NZ, OWN, KV), BF),
            pltpu.VMEM((KV, WIDTH), F32),
            pltpu.VMEM((2, 128, WIDTH), F32),
            pltpu.VMEM((ROWS_BLK, BAND, WIDTH), jnp.int32),
            pltpu.VMEM((ROWS_BLK, BAND, LANES), jnp.int32),
            pltpu.VMEM((NY, 64, LANES), BF),
            pltpu.VMEM((NXZ, 64, LANES), BF),
            dma((9 + n,)),
            dma(()),
            dma(()),
            dma((2,)),
            dma((2,)),
            dma((2,)),
            dma((2,)),
            dma((2,)),
            dma((2,)),
            dma((n,)),
            dma((n,)),
            dma((n, 2)),
            dma((n, 2)),
            dma((n, 2)),
            dma((n, 2)),
            dma((n, 2)),
            dma((n, 2)),
            dma((n, 2)),
            dma((n, 2)),
            dma((n, 2)),
            dma((n, 2)),
            dma((n, 4)),
            dma((n, 4)),
            dma((7,)),
            dma((7,)),
            dma((7,)),
            dma((7,)),
            pltpu.SemaphoreType.REGULAR,
        ],
        compiler_params=pltpu.CompilerParams(
            collective_id=0, has_side_effects=True, vmem_limit_bytes=48 * 1024 * 1024
        ),
        cost_estimate=pl.CostEstimate(flops=2_500_000_000, bytes_accessed=6_000_000, transcendentals=1280),
    )(
        hbm(tokens.reshape(NZ, 2, OWN, WIDTH)),
        hbm(key_weight),
        hbm(key_gain.reshape(1, KV)),
        hbm(cotangent.T),
        hbm(momentum),
        hbm(band_row),
        hbm(band_col),
        hbm(left),
        hbm(left_t),
        hbm(right),
    )


def solution(mesh):
    return jax.shard_map(
        on_device,
        mesh=mesh,
        in_specs=(
            P("dp", "mp"),
            P(None, "mp"),
            P(),
            P("dp", "mp"),
            P("dp", None, "mp"),
            P(None, "mp"),
            P(None, "mp"),
        ),
        out_specs=(P(None, "mp"), P("dp", None, "mp")),
        check_vma=False,
    )
```

```python
import math

import jax
import jax.numpy as jnp
import ml_dtypes
import numpy as np
from jax import lax
from jax.experimental import pallas as pl
from jax.experimental.pallas import tpu as pltpu
from jax.sharding import PartitionSpec as P

MESH = pl.DeviceIdType.MESH
BF = jnp.bfloat16
F32 = jnp.float32

SPAN = 64
BAND = 8
OFFSETS = 4
LOW = BAND * OFFSETS
EPS = 1e-06
DECAY = 0.9

NY = 8
NXZ = 8
NZ = 4
N_DP = NY * NXZ
OWN = 160
KV = 512
WIDTH = 640
ROWS_BLK = KV // SPAN
COLS_BLK = WIDTH // SPAN
LANES = 128
WINDOW = 3 * LANES
CHUNKS = ((0, 48), (48, 112))
FEATURES = (slice(0, 32), slice(32, 64))
WAYS = ((1, slice(0, 256)), (3, slice(256, 512)))


def split_const(table):
    high = table.astype(np.float32).astype(ml_dtypes.bfloat16)
    low = (table - high.astype(np.float64)).astype(np.float32).astype(ml_dtypes.bfloat16)
    return high.astype(np.float32), low.astype(np.float32)


def tables():
    f = np.arange(SPAN, dtype=np.float64)[:, None]
    n = np.arange(SPAN, dtype=np.float64)[None, :]
    c = np.cos(np.pi * (2.0 * n + 1.0) * f / (2.0 * SPAN))
    c = c * np.where(f == 0, np.sqrt(1.0 / SPAN), np.sqrt(2.0 / SPAN))
    c = c[:LOW]
    high, low = split_const(np.kron(np.eye(4), c))
    right = np.zeros((SPAN, OFFSETS, LANES // BAND, BAND))
    right[:] = c.T.reshape(SPAN, OFFSETS, 1, BAND)
    return (
        np.concatenate([high, low], axis=0),
        np.stack([np.ascontiguousarray(high.T), np.ascontiguousarray(low.T)]),
        np.stack(split_const(right.reshape(SPAN, OFFSETS * LANES))),
    )


def dot(a, b, dims=((1,), (0,))):
    return lax.dot_general(a, b, (dims, ((), ())), preferred_element_type=F32)


def split(value):
    high = value.astype(BF)
    return high, (value - high.astype(F32)).astype(BF)


def kernel(
    x_hbm, w_hbm, gain_hbm, cot_hbm, mom_hbm, row_hbm, col_hbm, left_hbm, left_t_hbm, right_hbm,
    upd_v, new_v,
    xv, wv, gain_ref, row_ref, col_ref, momv, left_f, left_t_f, right_f, leftv, left_tv, rightv,
    cot_in, cot_relay, cot_t, part_out, part_own, part_in, pair, relay, relay_sum, recv, dk, mom_new, sections,
    row_mask, col_mask, band_y, band_xz,
    load_sem, cs_s, cs_r, cr_s, cr_r, cf_s, cf_r, cz_s, cz_r, ps_s, ps_r, r1_s, r1_r, rd_s, rd_r, r2_s, r2_r, ag_s, ag_r, a2_s, a2_r, fw_s, fw_r,
    y_s, y_r, xz_s, xz_r, heard,
):
    dp = lax.axis_index("dp")
    mp = lax.axis_index("mp")
    zh = mp // 2
    core = mp % 2
    y = dp % NY
    xz = dp // NY
    sib = {"dp": dp, "mp": zh * 2 + (1 - core)}

    def z_peer(step):
        return {"dp": dp, "mp": ((zh + step) % NZ) * 2 + core}

    def y_peer(step):
        return {"dp": xz * NY + (y + step) % NY, "mp": mp}

    def xz_peer(step):
        return {"dp": ((xz + step) % NXZ) * NY + y, "mp": mp}

    barrier = pltpu.get_barrier_semaphore()
    def x_peer(step, flip):
        return {"dp": (((xz // 2 + step) % (NXZ // 2)) * 2 + (xz % 2 + flip) % 2) * NY + y, "mp": mp}

    near = [z_peer(1), z_peer(3), sib]
    far = [y_peer(s) for s in (2, 6, 1, 7)]
    far += [x_peer(2, 0), x_peer(1, 1), x_peer(3, 1), x_peer(1, 0), x_peer(3, 0), x_peer(0, 1)]

    def greet(peers):
        for peer in peers:
            pl.semaphore_signal(barrier, inc=1, device_id=peer, device_id_type=MESH)

    greet(near)
    loads = [pltpu.make_async_copy(w_hbm, wv, load_sem.at[0])]
    for k, (off, rows) in enumerate(CHUNKS):
        at = (slice(None), slice(None), pl.ds(off, rows))
        loads.append(pltpu.make_async_copy(x_hbm.at[at], xv.at[at], load_sem.at[1 + k]))
    base = 1 + len(CHUNKS)
    more = [(cot_hbm.at[:, pl.ds(pl.multiple_of((zh * 5 // 2) * LANES, LANES), WINDOW)], cot_in.at[zh, core]), (gain_hbm, gain_ref), (row_hbm, row_ref), (col_hbm, col_ref), (mom_hbm, momv)]
    more += [(left_hbm, left_f), (left_t_hbm, left_t_f), (right_hbm, right_f)]
    for k, (src, dst) in enumerate(more):
        loads.append(pltpu.make_async_copy(src, dst, load_sem.at[base + k]))
    for load in loads[: base + 1]:
        load.start()
    greet(far)
    for load in loads[base + 1 :]:
        load.start()

    def window(chip):
        return pl.ds(pl.multiple_of((chip * 5 // 2) * LANES, LANES), WINDOW)

    def remote(src, dst, send, recv_, peer):
        return pltpu.make_async_remote_copy(
            src_ref=src, dst_ref=dst, send_sem=send, recv_sem=recv_, device_id=peer, device_id_type=MESH
        )

    sent = []
    flying = {}

    def start(key, copy):
        copy.start()
        sent.append(copy)
        flying[key] = copy

    def landed(key, copy):
        copy.wait_recv()
        del flying[key]

    part_swaps = []

    def partial_keys(k, halves):
        off, rows = CHUNKS[k]
        at = pl.ds(off, rows)
        for side, place in halves:
            x_rows = xv[:, side, at, :].reshape(NZ * rows, WIDTH)
            part = dot(x_rows, wv[...], ((1,), (1,)))
            place[:, at, :] = part.astype(BF).reshape(NZ, rows, KV)

    def swap_parts(k):
        at = (slice(None), pl.ds(*CHUNKS[k]))
        part_swaps.append(remote(part_out.at[at], part_in.at[at], ps_s.at[k], ps_r.at[k], sib))
        start(("ps", k), part_swaps[k])

    loads[0].wait()
    away, stay = (1 - core, part_out), (core, part_own)
    loads[1].wait()
    partial_keys(0, (away, stay))
    pl.semaphore_wait(barrier, len(near) + len(far))
    for way, (step, half) in enumerate(WAYS):
        start(("cr", way), remote(
            cot_hbm.at[FEATURES[way], window((zh + 2) % NZ)], cot_relay.at[way], cr_s.at[way], cr_r.at[way], z_peer(step)
        ))
    for way, (step, half) in enumerate(WAYS):
        start(("cz", way), remote(
            cot_hbm.at[:, window((zh + step) % NZ)], cot_in.at[zh, core], cz_s.at[way], cz_r.at[way], z_peer(step)
        ))
    swap_parts(0)
    for k in range(1, len(CHUNKS)):
        loads[1 + k].wait()
        partial_keys(k, (away,))
        swap_parts(k)
    heralds = [y_peer(2), y_peer(6), x_peer(2, 0)]
    for peer in heralds:
        pl.semaphore_signal(heard, inc=1, device_id=peer, device_id_type=MESH)

    for k, (off, rows) in enumerate(CHUNKS):
        at = pl.ds(off, rows)
        if k > 0:
            partial_keys(k, (stay,))
        landed(("ps", k), part_swaps[k])
        pair[:, at, :] = (part_own[:, at, :].astype(F32) + part_in[:, at, :].astype(F32)).astype(BF)
        for way, (step, half) in enumerate(WAYS):
            start(("r1", k, way), remote(
                pair.at[(zh + 2) % NZ, at, half], relay.at[way, at], r1_s.at[k, way], r1_r.at[k, way], z_peer(step)
            ))

    for k, (off, rows) in enumerate(CHUNKS):
        at = pl.ds(off, rows)
        for way, (step, half) in enumerate(WAYS):
            other = WAYS[1 - way][1]
            start(("rd", k, way), remote(
                pair.at[(zh + step) % NZ, at, other], recv.at[way, at, other],
                rd_s.at[k, way], rd_r.at[k, way], z_peer(step),
            ))
    for load in loads[base + 1 :]:
        load.wait()
    mom_new[...] = DECAY * momv[0].astype(F32)
    leftv[...] = left_f[...].astype(BF)
    left_tv[...] = left_t_f[...].astype(BF)
    for way, (step, half) in enumerate(WAYS):
        landed(("cr", way), remote(cot_relay.at[way], cot_relay.at[way], cr_s.at[way], cr_r.at[way], sib))
        start(("cf", way), remote(
            cot_relay.at[way], cot_in.at[(zh + NZ - step) % NZ, core, FEATURES[way]], cf_s.at[way], cf_r.at[way], z_peer(step)
        ))
    for k, (off, rows) in enumerate(CHUNKS):
        at = pl.ds(off, rows)
        for way, (step, half) in enumerate(WAYS):
            landed(("r1", k, way), remote(
                pair.at[0, at, half], relay.at[way, at], r1_s.at[k, way], r1_r.at[k, way], sib
            ))
            both = pair[(zh + step) % NZ, at, half].astype(F32) + relay[way, at, :].astype(F32)
            relay_sum[way, at, :] = both.astype(BF)
            start(("r2", k, way), remote(
                relay_sum.at[way, at], recv.at[way, at, half], r2_s.at[k, way], r2_r.at[k, way], z_peer(step)
            ))

    block_r = lax.broadcasted_iota(jnp.int32, (BAND, WIDTH), 1) // SPAN
    block_c = lax.broadcasted_iota(jnp.int32, (BAND, LANES), 1) // BAND

    def spread(r, carry):
        of_row = jnp.zeros((BAND, WIDTH), jnp.int32)
        of_col = jnp.zeros((BAND, LANES), jnp.int32)
        for c in range(COLS_BLK):
            of_row = jnp.where(block_r == c, row_ref[r, c], of_row)
            of_col = jnp.where(block_c == c, col_ref[r, c], of_col)
        row_mask[r] = of_row
        col_mask[r] = of_col
        return carry

    lax.fori_loop(0, ROWS_BLK, spread, 0)
    loads[base].wait()
    for way, (step, half) in enumerate(WAYS):
        got = cot_in.at[(zh + NZ - step) % NZ, core]
        landed(("cz", way), remote(got, got, cz_s.at[way], cz_r.at[way], sib))
        got = cot_in.at[(zh + 2) % NZ, core, FEATURES[way]]
        landed(("cf", way), remote(got, got, cf_s.at[way], cf_r.at[way], sib))
    start(("cs",), remote(cot_in.at[:, core], cot_in.at[:, core], cs_s, cs_r, sib))
    landed(("cs",), remote(cot_in.at[:, 1 - core], cot_in.at[:, 1 - core], cs_s, cs_r, sib))
    cot_t[...] = cot_in[...].reshape(KV, WINDOW).T.astype(F32)
    cot_base = pl.multiple_of((zh % 2) * 64 + core * OWN, 32)
    gain = gain_ref[...]
    for k, (off, rows) in enumerate(CHUNKS):
        at = pl.ds(off, rows)
        for way, (step, half) in enumerate(WAYS):
            other = WAYS[1 - way][1]
            landed(("rd", k, way), remote(
                pair.at[0, at, other], recv.at[way, at, other], rd_s.at[k, way], rd_r.at[k, way], sib
            ))
        for way, (step, half) in enumerate(WAYS):
            landed(("r2", k, way), remote(
                relay_sum.at[way, at], recv.at[way, at, half], r2_s.at[k, way], r2_r.at[k, way], sib
            ))
        keys = pair[zh, at, :].astype(F32) + recv[0, at, :].astype(F32) + recv[1, at, :].astype(F32)
        scaled = gain * cot_t[pl.ds(cot_base + off, rows), :]
        inverse = lax.rsqrt(jnp.mean(keys * keys, axis=-1, keepdims=True) + EPS)
        inner = jnp.sum(scaled * keys, axis=-1, keepdims=True)
        dk[mp, at, :] = (inverse * scaled - (inverse * inverse * inverse * inner / KV) * keys).astype(BF)
        mine = dk.at[mp, at]
        for way, (step, half) in enumerate(WAYS):
            start(("ag", k, way), remote(mine, mine, ag_s.at[k, way], ag_r.at[k, way], z_peer(step)))
        start(("fw", k, 0), remote(mine, mine, fw_s.at[k, 0], fw_r.at[k, 0], sib))

    lane_block = (lax.broadcasted_iota(jnp.int32, (SPAN, OFFSETS * LANES), 1) % LANES) // BAND
    for c in range(COLS_BLK):
        for part in range(2):
            rightv[part, c * SPAN : (c + 1) * SPAN] = jnp.where(lane_block == c, right_f[part], 0.0).astype(BF)

    def owner(step, side):
        return ((zh + NZ - step) % NZ) * 2 + side

    for k, (off, rows) in enumerate(CHUNKS):
        at = pl.ds(off, rows)
        for way, (step, half) in enumerate(WAYS):
            got = dk.at[owner(step, core), at]
            landed(("ag", k, way), remote(got, got, ag_s.at[k, way], ag_r.at[k, way], sib))
            part = dk.at[owner(step, core), at, half]
            start(("a2", k, way), remote(part, part, a2_s.at[k, way], a2_r.at[k, way], z_peer(step)))
            start(("fw", k, step), remote(got, got, fw_s.at[k, step], fw_r.at[k, step], sib))
    def wait_other_core(k, step):
        got = dk.at[owner(step, 1 - core), pl.ds(*CHUNKS[k])]
        landed(("fw", k, step), remote(got, got, fw_s.at[k, step], fw_r.at[k, step], sib))

    def part_gradient(k, steps):
        off, rows = CHUNKS[k]
        chips = [(zh + NZ - step) % NZ for step in steps]
        some_dk = [dk[pl.ds(2 * chip, 2), pl.ds(off, rows), :].reshape(2 * rows, KV) for chip in chips]
        some_x = [xv[chip, :, pl.ds(off, rows), :].reshape(2 * rows, WIDTH) for chip in chips]
        some_dk, some_x = jnp.concatenate(some_dk, axis=0), jnp.concatenate(some_x, axis=0)
        return dot(some_dk, some_x, ((0,), (0,))) * (1.0 / math.sqrt(2 * NZ * OWN))

    last = len(CHUNKS) - 1
    for k in range(len(CHUNKS)):
        for step in (0, 1, 3):
            wait_other_core(k, step)
        mom_new[...] += part_gradient(k, (0, 1, 3))
    for k, (off, rows) in enumerate(CHUNKS):
        at = pl.ds(off, rows)
        for way, (step, half) in enumerate(WAYS):
            part = dk.at[owner(2, core), at, half]
            landed(("a2", k, way), remote(part, part, a2_s.at[k, way], a2_r.at[k, way], sib))
        got = dk.at[owner(2, core), at]
        start(("fw", k, 2), remote(got, got, fw_s.at[k, 2], fw_r.at[k, 2], sib))
        if k == last:
            for g in range(2):
                high, low = split(mom_new[g * 256 : (g + 1) * 256, :])
                both = dot(leftv[...], high)
                sections[g] = both[:128] + both[128:] + dot(leftv[:128], low)
        wait_other_core(k, 2)
        if k < last:
            mom_new[...] += part_gradient(k, (2,))
    last_piece = part_gradient(last, (2,))

    picked = []
    for g in range(2):
        both = dot(leftv[...], last_piece[g * 256 : (g + 1) * 256].astype(BF))
        sect = (sections[g] + both[:128] + both[128:]).reshape(4, OFFSETS, BAND, WIDTH)
        chosen = row_mask[g * 4 : (g + 1) * 4]
        total = jnp.zeros((4, BAND, WIDTH), F32)
        for band in range(OFFSETS):
            total = total + jnp.where(chosen == band, sect[:, band], 0.0)
        picked.append(total.reshape(32, WIDTH))
    sect = jnp.concatenate(picked, axis=0)
    high, low = split(sect)
    both = dot(jnp.concatenate([high, low], axis=0), rightv[0])
    full = both[:64] + both[64:] + dot(high, rightv[1])
    chosen = col_mask[...].reshape(64, LANES)
    coeffs = jnp.zeros((64, LANES), F32)
    for band in range(OFFSETS):
        coeffs = coeffs + jnp.where(chosen == band, full[:, band * LANES : (band + 1) * LANES], 0.0)

    band_y[y] = coeffs.astype(BF)
    pl.semaphore_wait(heard, len(heralds))
    for step in (4, 3, 5, 2, 6, 1, 7):
        start(("y", step), remote(band_y.at[y], band_y.at[y], y_s.at[step - 1], y_r.at[step - 1], y_peer(step)))

    mom_new[...] += last_piece
    def rebuild(values, exact, put):
        parts = [jnp.where(chosen == band, values, 0.0) for band in range(OFFSETS)]
        high, low = split(jnp.concatenate(parts, axis=1))
        if exact:
            both = dot(jnp.concatenate([high, low], axis=0), rightv[0], ((1,), (1,)))
            first = both[:64] + both[64:] + dot(high, rightv[1], ((1,), (1,)))
        else:
            first = dot(high, rightv[0], ((1,), (1,)))
        for g in range(2):
            rows = first[g * 32 : (g + 1) * 32].reshape(4, 1, BAND, WIDTH)
            bands = lax.broadcasted_iota(jnp.int32, (4, OFFSETS, BAND, WIDTH), 1)
            mask = row_mask[g * 4 : (g + 1) * 4].reshape(4, 1, BAND, WIDTH)
            spread_rows = jnp.where(mask == bands, rows, 0.0).reshape(128, WIDTH)
            high, low = split(spread_rows)
            out = dot(left_tv[0], high)
            if exact:
                out = out + dot(left_tv[1], high) + dot(left_tv[0], low)
            put(g, out)

    def put_new(g, own):
        at = slice(g * 256, (g + 1) * 256)
        new_v[0, at, :] = (mom_new[at, :] - own).astype(BF)

    rebuild(coeffs, True, put_new)

    for step in (1, 7, 2, 6, 3, 5, 4):
        got = band_y.at[(y + NY - step) % NY]
        landed(("y", step), remote(got, got, y_s.at[step - 1], y_r.at[step - 1], sib))
    total = band_y[0].astype(F32)
    for j in range(1, NY):
        total = total + band_y[j].astype(F32)
    band_xz[xz] = total.astype(BF)
    for step in (4, 3, 5, 2, 6, 1, 7):
        start(("xz", step), remote(band_xz.at[xz], band_xz.at[xz], xz_s.at[step - 1], xz_r.at[step - 1], xz_peer(step)))
    for step in range(1, NXZ):
        got = band_xz.at[(xz + NXZ - step) % NXZ]
        landed(("xz", step), remote(got, got, xz_s.at[step - 1], xz_r.at[step - 1], sib))
    total = band_xz[0].astype(F32)
    for j in range(1, NXZ):
        total = total + band_xz[j].astype(F32)

    def put_update(g, value):
        upd_v[g * 256 : (g + 1) * 256, :] = value.astype(BF)

    rebuild(total * (1.0 / N_DP), False, put_update)
    for copy in sent:
        copy.wait_send()


def hbm(value):
    return pltpu.with_memory_space_constraint(value, pltpu.HBM)


def on_device(tokens, key_weight, key_gain, cotangent, momentum, band_row, band_col):
    left, left_t, right = tables()
    n = len(CHUNKS)
    any_spec = pl.BlockSpec(memory_space=pltpu.HBM)
    vmem = pl.BlockSpec(memory_space=pltpu.VMEM)
    dma = pltpu.SemaphoreType.DMA
    return pl.pallas_call(
        kernel,
        out_shape=(
            jax.ShapeDtypeStruct((KV, WIDTH), BF),
            jax.ShapeDtypeStruct((1, KV, WIDTH), BF),
        ),
        in_specs=[any_spec] * 10,
        out_specs=(vmem, vmem),
        scratch_shapes=[
            pltpu.VMEM((NZ, 2, OWN, WIDTH), BF),
            pltpu.VMEM((KV, WIDTH), BF),
            pltpu.VMEM((1, KV), F32),
            pltpu.SMEM((ROWS_BLK, COLS_BLK), jnp.int32),
            pltpu.SMEM((ROWS_BLK, COLS_BLK), jnp.int32),
            pltpu.VMEM((1, KV, WIDTH), BF),
            pltpu.VMEM(left.shape, F32),
            pltpu.VMEM(left_t.shape, F32),
            pltpu.VMEM(right.shape, F32),
            pltpu.VMEM(left.shape, BF),
            pltpu.VMEM(left_t.shape, BF),
            pltpu.VMEM((2, WIDTH, OFFSETS * LANES), BF),
            pltpu.VMEM((NZ, 2, KV // (2 * NZ), WINDOW), BF),
            pltpu.VMEM((2, KV // (4 * NZ), WINDOW), BF),
            pltpu.VMEM((WINDOW, KV), F32),
            pltpu.VMEM((NZ, OWN, KV), BF),
            pltpu.VMEM((NZ, OWN, KV), BF),
            pltpu.VMEM((NZ, OWN, KV), BF),
            pltpu.VMEM((NZ, OWN, KV), BF),
            pltpu.VMEM((2, OWN, KV // 2), BF),
            pltpu.VMEM((2, OWN, KV // 2), BF),
            pltpu.VMEM((2, OWN, KV), BF),
            pltpu.VMEM((2 * NZ, OWN, KV), BF),
            pltpu.VMEM((KV, WIDTH), F32),
            pltpu.VMEM((2, 128, WIDTH), F32),
            pltpu.VMEM((ROWS_BLK, BAND, WIDTH), jnp.int32),
            pltpu.VMEM((ROWS_BLK, BAND, LANES), jnp.int32),
            pltpu.VMEM((NY, 64, LANES), BF),
            pltpu.VMEM((NXZ, 64, LANES), BF),
            dma((9 + n,)),
            dma(()),
            dma(()),
            dma((2,)),
            dma((2,)),
            dma((2,)),
            dma((2,)),
            dma((2,)),
            dma((2,)),
            dma((n,)),
            dma((n,)),
            dma((n, 2)),
            dma((n, 2)),
            dma((n, 2)),
            dma((n, 2)),
            dma((n, 2)),
            dma((n, 2)),
            dma((n, 2)),
            dma((n, 2)),
            dma((n, 2)),
            dma((n, 2)),
            dma((n, 4)),
            dma((n, 4)),
            dma((7,)),
            dma((7,)),
            dma((7,)),
            dma((7,)),
            pltpu.SemaphoreType.REGULAR,
        ],
        compiler_params=pltpu.CompilerParams(
            collective_id=0, has_side_effects=True, vmem_limit_bytes=48 * 1024 * 1024
        ),
        cost_estimate=pl.CostEstimate(flops=2_500_000_000, bytes_accessed=6_000_000, transcendentals=1280),
    )(
        hbm(tokens.reshape(NZ, 2, OWN, WIDTH)),
        hbm(key_weight),
        hbm(key_gain.reshape(1, KV)),
        hbm(cotangent.T),
        hbm(momentum),
        hbm(band_row),
        hbm(band_col),
        hbm(left),
        hbm(left_t),
        hbm(right),
    )


def solution(mesh):
    return jax.shard_map(
        on_device,
        mesh=mesh,
        in_specs=(
            P("dp", "mp"),
            P(None, "mp"),
            P(),
            P("dp", "mp"),
            P("dp", None, "mp"),
            P(None, "mp"),
            P(None, "mp"),
        ),
        out_specs=(P(None, "mp"), P("dp", None, "mp")),
        check_vma=False,
    )
```
